256 devices in a mesh: layer: 4 (over x_hi, core), slab: 64 (over z, y, x_lo).
Axes of the slice: x: 4 (x_hi: 2, x_lo: 2; x = x_hi * 2 + x_lo), y: 4, z: 8, core: 2. Of those that a mesh axis runs over, the one named last changes fastest.
Arguments:
- inputs: bfloat16 [4, 128, 3584], P('layer', 'slab'), may hold values from -6 to 6
- encoder: bfloat16 [4, 3584, 8192], P('layer', None, 'slab'), may hold values from -0.09375 to 0.09375
- active: int32 [4, 128, 8192], P('layer', None, 'slab'), may hold values 0 or 1
- decoder: bfloat16 [4, 4, 8192, 3584], P('layer', None, 'slab'), may hold values from -0.0625 to 0.0625
- goals: bfloat16 [7, 128, 3584], P(None, 'slab'), may hold values from -6 to 6
Outputs:
- grad_encoder: bfloat16 [4, 3584, 8192], P('layer', None, 'slab')
- grad_decoder: bfloat16 [4, 4, 8192, 3584], P('layer', None, 'slab')
The draws below stay inside these ranges and needn't reach their ends.
All inputs are finite; a program needn't handle non-finite values. No bound on the sum of `active` on one device may be relied on, other than what follows from the above.
Results may differ from the reference program's by a relative error of at most 0.013.
Values may be sent and summed in bfloat16 or wider, within the bound.
A program may use at most 64 MiB of HBM per device.

```python
import math
import jax
import jax.numpy as jnp

D = 3584
F = 8192
LAYERS = 4
TARGETS = 7
TOKENS = 128


def plant(result, rng, low, high):
    dims = result.shape
    index_at = [jax.random.randint(jax.random.fold_in(rng, axis), (), 0, dims[axis]) for axis in range(len(dims))]
    result = result.at[tuple(index_at)].set(low)
    longest = dims.index(max(dims))
    index_at[longest] = (index_at[longest] + 1) % dims[longest]
    return result.at[tuple(index_at)].set(high)


def levels(own_key, shape, split, smallest, top_value):
    factor_of, own = 1.0, jax.random.fold_in(own_key, 6)
    for axis_at, parts in split:
        steps = jnp.exp(jax.random.uniform(jax.random.fold_in(own, axis_at), (parts,), jnp.float32, smallest / len(split), top_value / len(split)))
        factor_of = factor_of * jnp.repeat(steps, shape[axis_at] // parts).reshape([-1 if axis == axis_at else 1 for axis in range(len(shape))])
    return factor_of


def bell_draw(stream_key, dims, deviation, reach, split=(), held_as=jnp.bfloat16):
    drawn = jax.random.normal(stream_key, dims, jnp.float32) * deviation
    if len(split) > 0:
        drawn = levels(stream_key, dims, split, -0.22, 0.18) * drawn
    return jnp.clip(drawn, min=-reach, max=reach).astype(held_as)


def setup_inputs(seed: int = 0) -> dict:
    streams_of = jax.random.split(jax.random.key(seed), 6)
    inputs = bell_draw(streams_of[0], (LAYERS, TOKENS, D), 1.0, 6.0, ((0, 4), (1, 64)))
    encoder = bell_draw(streams_of[1], (LAYERS, D, F), D ** -0.5, 0.09375, ((0, 4), (2, 64)))
    active = plant((jax.random.randint(streams_of[2], (LAYERS, TOKENS, F), 0, 4) < 1).astype(jnp.int32), jax.random.fold_in(streams_of[2], 1), 0, 1)
    decoder = bell_draw(streams_of[3], (LAYERS, LAYERS, F, D), F ** -0.5, 0.0625, ((0, 4), (2, 64)))
    goals = bell_draw(streams_of[4], (TARGETS, TOKENS, D), 1.0, 6.0, ((1, 64),))
    return {"inputs": inputs, "encoder": encoder, "active": active, "decoder": decoder, "goals": goals}


def reference(inputs, encoder, active, decoder, goals):
    scale = 1.0 / math.sqrt(TOKENS)
    latents_all = []
    for layer in range(LAYERS):
        pre = jnp.dot(inputs[layer], encoder[layer], preferred_element_type=jnp.float32)
        latents_all.append((active[layer].astype(jnp.float32) * pre).astype(jnp.bfloat16))
    recon = [jnp.zeros((TOKENS, D), jnp.float32) for target in range(TARGETS)]
    for layer in range(LAYERS):
        for offset in range(LAYERS):
            recon[layer + offset] = recon[layer + offset] + jnp.dot(latents_all[layer], decoder[layer, offset], preferred_element_type=jnp.float32)
    errors = [((recon[target] - goals[target].astype(jnp.float32)) * scale).astype(jnp.bfloat16) for target in range(TARGETS)]
    grad_enc_list = []
    grad_dec_list = []
    for layer in range(LAYERS):
        dec_row = []
        dlat = jnp.zeros((TOKENS, F), jnp.float32)
        for offset in range(LAYERS):
            err_here = errors[layer + offset]
            dec_row.append(jnp.dot(latents_all[layer].T, err_here, preferred_element_type=jnp.float32).astype(jnp.bfloat16))
            dlat = dlat + jnp.dot(err_here, decoder[layer, offset].T, preferred_element_type=jnp.float32)
        grad_dec_list.append(jnp.stack(dec_row))
        dpre = (active[layer].astype(jnp.float32) * dlat).astype(jnp.bfloat16)
        grad_enc_list.append(jnp.dot(inputs[layer].T, dpre, preferred_element_type=jnp.float32).astype(jnp.bfloat16))
    return (jnp.stack(grad_enc_list), jnp.stack(grad_dec_list))
```

```python
import math

import jax
import jax.numpy as jnp
from jax import lax
from jax.experimental import pallas as pl
from jax.experimental.pallas import tpu as pltpu
from jax.sharding import PartitionSpec as P

MESH = pl.DeviceIdType.MESH
F32, BF16 = jnp.float32, jnp.bfloat16

NZ, NG = 8, 8
TOK, D, FL = 128, 3584, 128
ROWS = 16
LANES = 128
TILES = D // LANES
NQ = 3
WIDE = 3 * LANES
XROWS = 64
MID, PAIR = 3, 2


def cols(tile, count=3):
    return pl.ds(pl.multiple_of(tile * LANES, LANES), count * LANES)


def kernel(
    inputs_ref,
    goals_ref,
    active_ref,
    enc_hbm,
    dec_hbm,
    genc_hbm,
    gdec_hbm,
    enc,
    dec,
    gdec,
    genc,
    xstage,
    xz,
    xwide,
    xb,
    xt,
    mask,
    lat_ref,
    latt_ref,
    dlat_ref,
    goal_block,
    sib_out,
    sib_in,
    part,
    part_in,
    zpart,
    zpart_in,
    xsum,
    xsum_in,
    err,
    err_sib,
    load_sem,
    out_sem,
    xz_send,
    xz_recv,
    xp_send,
    xp_recv,
    sib_send,
    sib_recv,
    part_send,
    part_recv,
    zp_send,
    zp_recv,
    xs_send,
    xs_recv,
    ez_send,
    ez_recv,
    ep_send,
    ep_recv,
    es_send,
    es_recv,
):
    layer = lax.axis_index("layer")
    slab = lax.axis_index("slab")
    x_hi, core = layer // 2, layer % 2
    z, g = slab // NG, slab % NG
    scale = 1.0 / math.sqrt(TOK)

    def z_peer(d):
        return (layer, ((z + d) % NZ) * NG + g)

    def g_peer(d):
        return (layer, z * NG + (g + d) % NG)

    sibling = (x_hi * 2 + 1 - core, slab)
    across = ((1 - x_hi) * 2 + core, slab)

    k_a = 3 * x_hi
    k_b = (layer + 2) % 4
    k_c = 3 - layer
    k_s = 1 + x_hi
    send_a = (core + x_hi + 1) % 2
    recv_a = 1 - send_a
    k_r = recv_a * k_a + (1 - recv_a) * k_b
    k_n = (1 - recv_a) * k_a + recv_a * k_b
    z_s, z_r, z_n = 5 * (1 - send_a), 5 * (1 - recv_a), 5 * recv_a

    def tile_of(zz, q, is_a):
        return 9 * zz + 3 * q - 44 * (1 - is_a)

    enc_copy = pltpu.make_async_copy(enc_hbm.at[0], enc, load_sem.at[0])
    dec_copy = pltpu.make_async_copy(dec_hbm.at[0], dec, load_sem.at[1])
    enc_copy.start()
    dec_copy.start()

    barrier = pltpu.get_barrier_semaphore()

    @pl.loop(1, 8)
    def _(d):
        pl.semaphore_signal(barrier, inc=1, device_id=z_peer(d), device_id_type=MESH)
        pl.semaphore_signal(barrier, inc=1, device_id=g_peer(d), device_id_type=MESH)

    pl.semaphore_signal(barrier, inc=1, device_id=sibling, device_id_type=MESH)
    pl.semaphore_signal(barrier, inc=1, device_id=across, device_id_type=MESH)

    xstage[...] = jnp.zeros_like(xstage)
    for c in range(TILES):
        xstage[2 * c : 2 * c + 2, :] = inputs_ref[0, :, c * LANES : (c + 1) * LANES].astype(F32)
    xz[z] = xstage[...].astype(BF16)

    pl.semaphore_wait(barrier, 16)

    def send(src, dst, ssem, rsem, device):
        pltpu.make_async_remote_copy(
            src_ref=src, dst_ref=dst, send_sem=ssem, recv_sem=rsem, device_id=device, device_id_type=MESH
        ).start()

    def wait(ref, sem):
        pltpu.make_async_copy(ref, ref, sem).wait()

    @pl.loop(1, 8)
    def _(d):
        send(xz.at[z], xz.at[z], xz_send, xz_recv, z_peer(d))

    for gg in range(NG):
        for r in range(2):
            mask[gg * ROWS + r * 8 : gg * ROWS + r * 8 + 8, :] = active_ref[
                0, pl.ds(gg * 2 + r, 8, stride=16), :
            ].astype(F32)

    mine = lax.broadcasted_iota(jnp.int32, (8, 1), 0) == z
    first_half = (1 - x_hi).astype(F32)

    def goal_rows(target, tile, count, factor):
        pair = goals_ref[target, :, cols(tile, count)].astype(F32) * factor
        zero = jnp.zeros((8, count * LANES), F32)
        return jnp.concatenate([jnp.where(mine, pair[r : r + 1], zero) for r in range(2)], axis=0)

    one = jnp.float32(1.0)
    t_a, t_b = 5 * x_hi + core, 2 + 2 * core
    for q in range(NQ):
        for zz in range(3):
            goal_block[q, zz] = goal_rows(t_a, 9 * zz + 3 * q, 3, one)
            goal_block[q, zz + 5] = goal_rows(t_b, 9 * (zz + 5) + 3 * q - 44, 3, first_half)
        goal_block[q, MID] = goal_rows(3, core * 14 + 3 * q, 3, first_half)
        if q == 0:
            goal_block[q, MID + 1] = goal_rows(3, core * 14 + 9, 3, first_half)
        else:
            goal_block[q, MID + 1] = jnp.zeros((ROWS, WIDE), F32)
            if q == 1:
                goal_block[q, MID + 1, :, 0 : 2 * LANES] = goal_rows(3, core * 14 + 12, 2, first_half)
            else:
                goal_block[q, MID + 1, :, 0:LANES] = goal_rows(t_a, 27, 1, one)
                goal_block[q, MID + 1, :, LANES : 2 * LANES] = goal_rows(t_b, 0, 1, first_half)

    wait(xz.at[pl.ds(0, 7)], xz_recv)
    for zz in range(NZ):
        xwide[zz * XROWS : (zz + 1) * XROWS, :] = xz[zz].astype(F32)
    for c in range(TILES):
        xb[g, :, c * LANES : (c + 1) * LANES] = jnp.concatenate(
            [xwide[pl.ds(2 * c + r, 8, stride=XROWS), :] for r in range(2)], axis=0
        ).astype(BF16)

    @pl.loop(1, 8)
    def _(d):
        send(xb.at[g], xb.at[g], xp_send, xp_recv, g_peer(d))

    enc_copy.wait()
    dec_copy.wait()
    wait(xb.at[pl.ds(0, 7)], xp_recv)

    pre = jnp.dot(xb[...].reshape(TOK, D), enc[...], preferred_element_type=F32)
    act = mask[...] * pre
    lat_ref[...] = act.astype(BF16)
    latt_ref[...] = act.T.astype(BF16)

    def decoded(k, tile, count=3):
        return jnp.dot(lat_ref[...], dec[k, :, cols(tile, count)], preferred_element_type=F32)

    def blocks(value):
        return value.reshape(NG, ROWS, value.shape[-1])

    zeros = jnp.zeros((NG, ROWS, LANES), BF16)
    other = (1 - core) * 14
    own = core * 14
    is_a, is_b = send_a.astype(F32), (1 - send_a).astype(F32)

    for q in range(NQ):

        @pl.loop(0, 3)
        def _(i):
            sib_out[q, i] = blocks(decoded(k_s, tile_of(z_s + i, q, send_a)).astype(BF16))

        sib_out[q, 3] = blocks(decoded(k_c, other + 3 * q).astype(BF16))
        if q == 0:
            sib_out[q, 4] = blocks(decoded(k_c, other + 9).astype(BF16))
        elif q == 1:
            sib_out[q, 4, :, :, 0 : 2 * LANES] = blocks(decoded(k_c, other + 12, 2).astype(BF16))
            sib_out[q, 4, :, :, 2 * LANES :] = zeros
        else:
            sib_out[q, 4, :, :, 0:LANES] = blocks((decoded(k_s, 27, 1) * is_a).astype(BF16))
            sib_out[q, 4, :, :, LANES : 2 * LANES] = blocks((decoded(k_s, 0, 1) * is_b).astype(BF16))
            sib_out[q, 4, :, :, 2 * LANES :] = zeros
        send(sib_out.at[q], sib_in.at[q], sib_send.at[q], sib_recv.at[q], sibling)

    for q in range(NQ):

        @pl.loop(0, 3)
        def _(i):
            part[q, :, z_n + i] = blocks(decoded(k_n, tile_of(z_n + i, q, 1 - recv_a)).astype(BF16))

        wait(sib_in.at[q], sib_recv.at[q])

        @pl.loop(0, 3)
        def _(i):
            part[q, :, z_r + i] = (
                blocks(decoded(k_r, tile_of(z_r + i, q, recv_a))) + sib_in[q, i].astype(F32)
            ).astype(BF16)

        part[q, :, MID] = (blocks(decoded(k_c, own + 3 * q)) + sib_in[q, 3].astype(F32)).astype(BF16)

        def last(lanes, value):
            part[q, :, MID + 1, :, lanes] = (
                blocks(value) + sib_in[q, 4, :, :, lanes].astype(F32)
            ).astype(BF16)

        if q == 0:
            last(slice(0, WIDE), decoded(k_c, own + 9))
        elif q == 1:
            last(slice(0, 2 * LANES), decoded(k_c, own + 12, 2))
            part[q, :, MID + 1, :, 2 * LANES :] = zeros
        else:
            last(slice(0, LANES), decoded(k_a, 27, 1))
            last(slice(LANES, 2 * LANES), decoded(k_b, 0, 1))
            part[q, :, MID + 1, :, 2 * LANES :] = zeros

        @pl.loop(1, 8)
        def _(d):
            send(part.at[q, (g + d) % NG], part_in.at[q, d - 1], part_send.at[q], part_recv.at[q], g_peer(d))

    for c in range(TILES):
        block = xb[:, :, c * LANES : (c + 1) * LANES].reshape(TOK, LANES)
        xt[c * LANES : (c + 1) * LANES, :] = block.T

    def plane_sum(q):
        wait(part_in.at[q], part_recv.at[q])

        @pl.loop(0, NZ)
        def _(zz):
            total = part[q, g, zz].astype(F32) - goal_block[q, zz]
            for d in range(7):
                total = total + part_in[q, d, zz].astype(F32)
            zpart[q, zz] = total.astype(BF16)

        @pl.loop(1, 8)
        def _(d):
            send(zpart.at[q, (z + d) % NZ], zpart_in.at[q, d - 1], zp_send.at[q], zp_recv.at[q], z_peer(d))

    def z_sum(q):
        wait(zpart_in.at[q], zp_recv.at[q])
        total = zpart[q, z].astype(F32)
        for d in range(7):
            total = total + zpart_in[q, d].astype(F32)
        xsum[q] = total
        send(xsum.at[q], xsum_in.at[q], xs_send.at[q], xs_recv.at[q], across)

    def x_sum(q):
        wait(xsum_in.at[q], xs_recv.at[q])
        shared = z >= 3
        if q == 2:
            lane = lax.broadcasted_iota(jnp.int32, (ROWS, WIDE), 1)
            private = jnp.logical_or(z < 3, jnp.logical_and(z == 4, lane < LANES))
            shared = jnp.logical_not(private)
        total = xsum[q] + jnp.where(shared, xsum_in[q], 0.0)
        err[q, g, z] = (total * scale).astype(BF16)

        @pl.loop(1, 8)
        def _(d):
            send(err.at[q, g, z], err.at[q, g, z], ez_send.at[q], ez_recv.at[q], z_peer(d))

    def z_spread(q):
        wait(err.at[q, g, pl.ds(0, 7)], ez_recv.at[q])

        @pl.loop(1, 8)
        def _(d):
            send(err.at[q, g], err.at[q, g], ep_send.at[q], ep_recv.at[q], g_peer(d))

    plane_sum(0)
    z_sum(0)
    plane_sum(1)
    x_sum(0)
    z_sum(1)
    plane_sum(2)
    z_spread(0)
    x_sum(1)
    z_sum(2)
    z_spread(1)
    x_sum(2)
    z_spread(2)

    dlat_ref[...] = jnp.zeros_like(dlat_ref)

    def backward(error, k, tile, count=3):
        where = cols(tile, count)
        dlat_ref[...] += lax.dot_general(
            error, dec[k, :, where], (((1,), (1,)), ((), ())), preferred_element_type=F32
        )
        gdec[k, :, where] = jnp.dot(latt_ref[...], error, preferred_element_type=F32).astype(BF16)

    def whole(value):
        return value.reshape(TOK, value.shape[-1])

    for q in range(NQ):
        wait(err.at[q, pl.ds(0, 7)], ep_recv.at[q])
        send(err.at[q, :, pl.ds(z_r, 3)], err_sib.at[q, :, pl.ds(0, 3)], es_send.at[q], es_recv.at[q], sibling)
        send(err.at[q, :, pl.ds(3, 2)], err_sib.at[q, :, pl.ds(3, 2)], es_send.at[q], es_recv.at[q], sibling)

        @pl.loop(0, 3)
        def _(i):
            backward(whole(err[q, :, i]), k_a, tile_of(i, q, 1))
            backward(whole(err[q, :, 5 + i]), k_b, tile_of(5 + i, q, 0))

        backward(whole(err[q, :, MID]), k_c, own + 3 * q)
        if q == 0:
            backward(whole(err[q, :, MID + 1]), k_c, own + 9)
        elif q == 1:
            backward(whole(err[q, :, MID + 1, :, 0 : 2 * LANES]), k_c, own + 12, 2)
        else:
            backward(whole(err[q, :, MID + 1, :, 0:LANES]), k_a, 27, 1)
            backward(whole(err[q, :, MID + 1, :, LANES : 2 * LANES]), k_b, 0, 1)

    for q in range(NQ):
        wait(err_sib.at[q], es_recv.at[q])

        @pl.loop(0, 3)
        def _(i):
            backward(whole(err_sib[q, :, i]), k_s, tile_of(z_s + i, q, send_a))

        backward(whole(err_sib[q, :, 3]), k_c, other + 3 * q)
        if q == 0:
            backward(whole(err_sib[q, :, 4]), k_c, other + 9)
        elif q == 1:
            backward(whole(err_sib[q, :, 4, :, 0 : 2 * LANES]), k_c, other + 12, 2)
        else:
            lanes = pl.ds(pl.multiple_of((1 - send_a) * LANES, LANES), LANES)
            backward(whole(err_sib[q, :, 4, :, lanes]), k_s, 27 * send_a, 1)

    gdec_copy = pltpu.make_async_copy(gdec, gdec_hbm.at[0], out_sem.at[0])
    gdec_copy.start()
    dpre = (mask[...] * dlat_ref[...]).astype(BF16)
    genc[...] = jnp.dot(xt[...], dpre, preferred_element_type=F32).astype(BF16)
    genc_copy = pltpu.make_async_copy(genc, genc_hbm.at[0], out_sem.at[1])
    genc_copy.start()

    wait(xz.at[pl.ds(0, 7)], xz_send)
    wait(xb.at[pl.ds(0, 7)], xp_send)
    for q in range(NQ):
        wait(sib_in.at[q], sib_send.at[q])
        wait(part_in.at[q], part_send.at[q])
        wait(zpart_in.at[q], zp_send.at[q])
        wait(xsum_in.at[q], xs_send.at[q])
        wait(zpart_in.at[q], ez_send.at[q])
        wait(err.at[q, pl.ds(0, 7)], ep_send.at[q])
        wait(err_sib.at[q], es_send.at[q])
    gdec_copy.wait()
    genc_copy.wait()


def local(inputs, encoder, active, decoder, goals):
    vmem = pl.BlockSpec(memory_space=pltpu.VMEM)
    hbm = pl.BlockSpec(memory_space=pl.ANY)
    dma = pltpu.SemaphoreType.DMA
    per_q = [dma((NQ,))] * 2
    return pl.pallas_call(
        kernel,
        out_shape=(
            jax.ShapeDtypeStruct((1, D, FL), BF16),
            jax.ShapeDtypeStruct((1, 4, FL, D), BF16),
        ),
        in_specs=[vmem, vmem, vmem, hbm, hbm],
        out_specs=(hbm, hbm),
        scratch_shapes=[
            pltpu.VMEM((D, FL), BF16),
            pltpu.VMEM((4, FL, D), BF16),
            pltpu.VMEM((4, FL, D), BF16),
            pltpu.VMEM((D, FL), BF16),
            pltpu.VMEM((XROWS, LANES), F32),
            pltpu.VMEM((NZ, XROWS, LANES), BF16),
            pltpu.VMEM((NZ * XROWS, LANES), F32),
            pltpu.VMEM((NG, ROWS, D), BF16),
            pltpu.VMEM((D, TOK), BF16),
            pltpu.VMEM((TOK, FL), F32),
            pltpu.VMEM((TOK, FL), BF16),
            pltpu.VMEM((FL, TOK), BF16),
            pltpu.VMEM((TOK, FL), F32),
            pltpu.VMEM((NQ, NZ, ROWS, WIDE), F32),
            pltpu.VMEM((NQ, 5, NG, ROWS, WIDE), BF16),
            pltpu.VMEM((NQ, 5, NG, ROWS, WIDE), BF16),
            pltpu.VMEM((NQ, NG, NZ, ROWS, WIDE), BF16),
            pltpu.VMEM((NQ, NG - 1, NZ, ROWS, WIDE), BF16),
            pltpu.VMEM((NQ, NZ, ROWS, WIDE), BF16),
            pltpu.VMEM((NQ, NZ - 1, ROWS, WIDE), BF16),
            pltpu.VMEM((NQ, ROWS, WIDE), F32),
            pltpu.VMEM((NQ, ROWS, WIDE), F32),
            pltpu.VMEM((NQ, NG, NZ, ROWS, WIDE), BF16),
            pltpu.VMEM((NQ, NG, 5, ROWS, WIDE), BF16),
            dma((2,)),
            dma((2,)),
            dma,
            dma,
            dma,
            dma,
            *per_q,
            *per_q,
            *per_q,
            *per_q,
            *per_q,
            *per_q,
            *per_q,
        ],
        compiler_params=pltpu.CompilerParams(
            collective_id=0, has_side_effects=True, vmem_limit_bytes=56 * 2**20
        ),
        name="step",
    )(inputs, goals, active, encoder, decoder)


def solution(mesh):
    return jax.shard_map(
        local,
        mesh=mesh,
        in_specs=(
            P("layer", "slab", None),
            P("layer", None, "slab"),
            P("layer", None, "slab"),
            P("layer", None, "slab", None),
            P(None, "slab", None),
        ),
        out_specs=(P("layer", None, "slab"), P("layer", None, "slab", None)),
        check_vma=False,
    )
```

```python
import math

import jax
import jax.numpy as jnp
from jax import lax
from jax.experimental import pallas as pl
from jax.experimental.pallas import tpu as pltpu
from jax.sharding import PartitionSpec as P

MESH = pl.DeviceIdType.MESH
F32, BF16 = jnp.float32, jnp.bfloat16

NZ, NG = 8, 8
TOK, D, FL = 128, 3584, 128
ROWS = 16
LANES = 128
TILES = D // LANES
NQ = 3
WIDE = 3 * LANES
XROWS = 64
MID = 3
FAR_FIRST = (4, 3, 5, 2, 6, 1, 7, 0)


def cols(tile, count=3):
    return pl.ds(pl.multiple_of(tile * LANES, LANES), count * LANES)


def kernel(
    inputs_hbm,
    goals_hbm,
    active_hbm,
    enc_hbm,
    dec_hbm,
    gdec,
    xt,
    mask,
    dlat_ref,
    inputs_ref,
    goals_ref,
    active_ref,
    enc,
    dec,
    xstage,
    xz,
    xwide,
    xb,
    lat_ref,
    latt_ref,
    goal_block,
    sib_out,
    sib_in,
    part,
    y_in,
    z_in,
    err,
    err_far,
    err_sib,
    load_sem,
    xz_send,
    xz_recv,
    xb_send,
    xb_recv,
    sib_send,
    sib_recv,
    y_send,
    y_recv,
    z_send,
    z_recv,
    ez_send,
    ez_recv,
    ef_send,
    ef_recv,
    ep_send,
    ep_recv,
    es_send,
    es_recv,
):
    layer = lax.axis_index("layer")
    slab = lax.axis_index("slab")
    x_hi, core = layer // 2, layer % 2
    z, g = slab // NG, slab % NG
    y, x = g // 2, g % 2
    y1, y2, y3 = (y + 1) % 4, (y + 2) % 4, (y + 3) % 4
    keep = (x + x_hi) % 2
    g_keep, g_pass = y * 2 + keep, y * 2 + 1 - keep
    scale = 1.0 / math.sqrt(TOK)

    def z_peer(d):
        return (layer, ((z + d) % NZ) * NG + g)

    def pair_z(d):
        return (layer, ((z + d) % NZ) * NG + y * 2 + 1 - x)

    def across_z(d):
        return ((1 - x_hi) * 2 + core, ((z + d) % NZ) * NG + y * 2 + 1 - x)

    right = (layer, z * NG + y1 * 2 + x)
    left = (layer, z * NG + y3 * 2 + x)
    pair = (layer, z * NG + y * 2 + 1 - x)
    sibling = (x_hi * 2 + 1 - core, slab)
    right_pair = (layer, z * NG + y1 * 2 + 1 - x)
    left_pair = (layer, z * NG + y3 * 2 + 1 - x)

    k_a = 3 * x_hi
    k_b = (layer + 2) % 4
    k_c = 3 - layer
    k_s = 1 + x_hi
    send_a = (core + x_hi + 1) % 2
    recv_a = 1 - send_a
    k_r = recv_a * k_a + (1 - recv_a) * k_b
    k_n = (1 - recv_a) * k_a + recv_a * k_b
    z_s, z_r, z_n = 5 * (1 - send_a), 5 * (1 - recv_a), 5 * recv_a

    def first_tile(q, is_a):
        return 9 * q + 1 - is_a

    loads = [
        pltpu.make_async_copy(src, dst, load_sem.at[i])
        for i, (src, dst) in enumerate(
            [
                (inputs_hbm.at[0], inputs_ref),
                (active_hbm.at[0], active_ref),
                (goals_hbm, goals_ref),
                (enc_hbm.at[0], enc),
                (dec_hbm.at[0], dec),
            ]
        )
    ]
    for load in loads:
        load.start()

    barrier = pltpu.get_barrier_semaphore()

    def greet(device):
        pl.semaphore_signal(barrier, inc=1, device_id=device, device_id_type=MESH)

    for d in FAR_FIRST:
        greet(across_z(d))
        greet(pair_z(d))
        if d:
            greet(z_peer(d))
    for device in (right, left, right_pair, left_pair, sibling):
        greet(device)

    xstage[...] = jnp.zeros_like(xstage)
    loads[0].wait()
    for c in range(TILES):
        xstage[2 * c : 2 * c + 2, :] = inputs_ref[:, c * LANES : (c + 1) * LANES].astype(F32)
    xz[z] = xstage[...].astype(BF16)

    pl.semaphore_wait(barrier, 28)

    def send(src, dst, ssem, rsem, device):
        pltpu.make_async_remote_copy(
            src_ref=src, dst_ref=dst, send_sem=ssem, recv_sem=rsem, device_id=device, device_id_type=MESH
        ).start()

    def wait(ref, sem):
        pltpu.make_async_copy(ref, ref, sem).wait()

    class Spread:
        def __init__(self, buf, half, near, mate, ssem, rsem):
            self.buf, self.half, self.near, self.mate = buf, half, near, mate
            self.ssem, self.rsem = ssem, rsem

        def put(self, block, slot, device):
            send(self.buf.at[block], self.buf.at[block], self.ssem, self.rsem(slot), device)

        def put_half(self, block, i, slot, device):
            part_of = self.half(block, i)
            send(part_of, part_of, self.ssem, self.rsem(slot), device)

        def got(self, slot):
            wait(self.buf.at[0], self.rsem(slot))

        def start(self):
            own = y * 2 + self.near
            self.put(own, 1, right)
            self.put(own, 2, left)
            self.put(own, 3, right_pair)
            self.put(own, 4, left_pair)
            self.put(own, 0, pair)

        def onward(self, which, slot):
            self.got(slot)
            self.put_half(y3 * 2 + which, 0, slot + 4, right)
            self.got(slot + 1)
            self.put_half(y1 * 2 + which, 1, slot + 5, left)

        def second(self):
            self.onward(self.near, 1)

        def third(self):
            self.onward(self.mate, 3)

        def finish(self):
            self.got(0)
            for slot in range(5, 9):
                wait(self.half(0, 0), self.rsem(slot))

        def left_here(self):
            wait(self.buf.at[pl.ds(0, 7)], self.ssem)

    for d in FAR_FIRST[:7]:
        send(xz.at[z], xz.at[z], xz_send, xz_recv, z_peer(d))

    loads[1].wait()
    for gg in range(NG):
        for r in range(2):
            mask[gg * ROWS + r * 8 : gg * ROWS + r * 8 + 8, :] = active_ref[
                pl.ds(gg * 2 + r, 8, stride=16), :
            ].astype(F32)

    mine = lax.broadcasted_iota(jnp.int32, (8, 1), 0) == z
    loads[2].wait()

    first_half = (1 - x_hi).astype(F32)

    def goal_rows(target, tile, count, factor=first_half):
        two = goals_ref[target, :, cols(tile, count)].astype(F32) * factor
        zero = jnp.zeros((8, count * LANES), F32)
        return jnp.concatenate([jnp.where(mine, two[r : r + 1], zero) for r in range(2)], axis=0)

    t_a, t_b = 5 * x_hi + core, 2 + 2 * core
    for q in range(NQ):
        for zz in range(3):
            goal_block[q, zz] = goal_rows(t_a, 9 * q + 3 * zz, 3, 1.0)
            goal_block[q, zz + 5] = goal_rows(t_b, 9 * q + 3 * zz + 1, 3)
        goal_block[q, MID] = goal_rows(3, core * 14 + 3 * q, 3)
        if q == 0:
            goal_block[q, MID + 1] = goal_rows(3, core * 14 + 9, 3)
        else:
            goal_block[q, MID + 1] = jnp.zeros((ROWS, WIDE), F32)
            if q == 1:
                goal_block[q, MID + 1, :, 0 : 2 * LANES] = goal_rows(3, core * 14 + 12, 2)
            else:
                goal_block[q, MID + 1, :, 0:LANES] = goal_rows(t_a, 27, 1, 1.0)
                goal_block[q, MID + 1, :, LANES : 2 * LANES] = goal_rows(t_b, 0, 1)

    wait(xz.at[pl.ds(0, 7)], xz_recv)
    for zz in range(NZ):
        xwide[zz * XROWS : (zz + 1) * XROWS, :] = xz[zz].astype(F32)
    for c in range(TILES):
        xb[g, c // 14, :, (c % 14) * LANES : (c % 14 + 1) * LANES] = jnp.concatenate(
            [xwide[pl.ds(2 * c + r, 8, stride=XROWS), :] for r in range(2)], axis=0
        ).astype(BF16)

    x_spread = Spread(xb, lambda b, i: xb.at[b, i], x, 1 - x, xb_send, lambda slot: xb_recv.at[slot])
    x_spread.start()
    x_spread.second()
    x_spread.third()
    loads[3].wait()
    loads[4].wait()
    x_spread.finish()

    pre = jnp.dot(xb[:, 0].reshape(TOK, D // 2), enc[: D // 2, :], preferred_element_type=F32)
    pre = pre + jnp.dot(xb[:, 1].reshape(TOK, D // 2), enc[D // 2 :, :], preferred_element_type=F32)
    act = mask[...] * pre
    lat_ref[...] = act.astype(BF16)
    latt_ref[...] = act.T.astype(BF16)

    def decoded(k, tile, count=3):
        return jnp.dot(lat_ref[...], dec[k, :, cols(tile, count)], preferred_element_type=F32)

    def blocks(value):
        return value.reshape(NG, ROWS, value.shape[-1])

    zeros = jnp.zeros((NG, ROWS, LANES), BF16)
    other = (1 - core) * 14
    own = core * 14
    is_a, is_b = send_a.astype(F32), (1 - send_a).astype(F32)

    def for_sibling(q):
        wide = decoded(k_s, first_tile(q, send_a), 9).astype(BF16)
        for i in range(3):
            sib_out[q, i] = blocks(wide[:, i * WIDE : (i + 1) * WIDE])

        sib_out[q, 3] = blocks(decoded(k_c, other + 3 * q).astype(BF16))
        if q == 0:
            sib_out[q, 4] = blocks(decoded(k_c, other + 9).astype(BF16))
        elif q == 1:
            sib_out[q, 4, :, :, 0 : 2 * LANES] = blocks(decoded(k_c, other + 12, 2).astype(BF16))
            sib_out[q, 4, :, :, 2 * LANES :] = zeros
        else:
            sib_out[q, 4, :, :, 0:LANES] = blocks((decoded(k_s, 27, 1) * is_a).astype(BF16))
            sib_out[q, 4, :, :, LANES : 2 * LANES] = blocks((decoded(k_s, 0, 1) * is_b).astype(BF16))
            sib_out[q, 4, :, :, 2 * LANES :] = zeros
        send(sib_out.at[q], sib_in.at[q], sib_send.at[q], sib_recv.at[q], sibling)

    def own_alone(q):
        wide = decoded(k_n, first_tile(q, 1 - recv_a), 9).astype(BF16)
        for i in range(3):
            part[q, :, z_n + i] = blocks(wide[:, i * WIDE : (i + 1) * WIDE])

    def own_shared(q):
        wait(sib_in.at[q], sib_recv.at[q])

        wide = decoded(k_r, first_tile(q, recv_a), 9)
        for i in range(3):
            part[q, :, z_r + i] = (
                blocks(wide[:, i * WIDE : (i + 1) * WIDE]) + sib_in[q, i].astype(F32)
            ).astype(BF16)

        part[q, :, MID] = (blocks(decoded(k_c, own + 3 * q)) + sib_in[q, 3].astype(F32)).astype(BF16)

        def last(lanes, value):
            part[q, :, MID + 1, :, lanes] = (
                blocks(value) + sib_in[q, 4, :, :, lanes].astype(F32)
            ).astype(BF16)

        if q == 0:
            last(slice(0, WIDE), decoded(k_c, own + 9))
        elif q == 1:
            last(slice(0, 2 * LANES), decoded(k_c, own + 12, 2))
            part[q, :, MID + 1, :, 2 * LANES :] = zeros
        else:
            last(slice(0, LANES), decoded(k_a, 27, 1))
            last(slice(LANES, 2 * LANES), decoded(k_b, 0, 1))
            part[q, :, MID + 1, :, 2 * LANES :] = zeros

    def y_first(q):
        ss = y_send.at[q]
        send(part.at[q, y2 * 2], y_in.at[q, 0], ss, y_recv.at[q, 0], right)
        send(part.at[q, y2 * 2 + 1], y_in.at[q, 1], ss, y_recv.at[q, 1], left)
        send(part.at[q, y1 * 2 + 1], y_in.at[q, 2], ss, y_recv.at[q, 2], right)
        send(part.at[q, y3 * 2], y_in.at[q, 3], ss, y_recv.at[q, 2], left)

    def y_second(q):
        ss = y_send.at[q]
        wait(y_in.at[q, 0], y_recv.at[q, 0])
        for zz in range(NZ):
            part[q, y1 * 2, zz] = (part[q, y1 * 2, zz].astype(F32) + y_in[q, 0, zz].astype(F32)).astype(BF16)
        send(part.at[q, y1 * 2], y_in.at[q, 4], ss, y_recv.at[q, 2], right)
        wait(y_in.at[q, 1], y_recv.at[q, 1])
        for zz in range(NZ):
            part[q, y3 * 2 + 1, zz] = (
                part[q, y3 * 2 + 1, zz].astype(F32) + y_in[q, 1, zz].astype(F32)
            ).astype(BF16)
        send(part.at[q, y3 * 2 + 1], y_in.at[q, 5], ss, y_recv.at[q, 2], left)

    def y_sum(q):
        wait(y_in.at[q, pl.ds(0, 4)], y_recv.at[q, 2])
        for half, (one, two) in enumerate(((3, 4), (2, 5))):
            here = (x == half).astype(F32)
            for zz in range(NZ):
                part[q, y * 2 + half, zz] = (
                    part[q, y * 2 + half, zz].astype(F32)
                    + y_in[q, one, zz].astype(F32)
                    + y_in[q, two, zz].astype(F32)
                    - goal_block[q, zz] * here
                ).astype(BF16)
        for d in FAR_FIRST:
            zd = (z + d) % NZ
            send(part.at[q, g_pass, zd], z_in.at[q, 7 + d], z_send.at[q], z_recv.at[q], pair_z(d))
            if d:
                send(part.at[q, g_keep, zd], z_in.at[q, d - 1], z_send.at[q], z_recv.at[q], z_peer(d))

    def z_sum(q):
        wait(z_in.at[q], z_recv.at[q])
        total = part[q, g_keep, z].astype(F32)
        for i in range(15):
            total = total + z_in[q, i].astype(F32)
        err[q, g_keep, z] = (total * scale).astype(BF16)
        own = err.at[q, g_keep, z]
        for d in FAR_FIRST[:7]:
            send(own, own, ez_send.at[q], ez_recv.at[q], z_peer(d))

        @pl.when(z >= 3)
        def _():
            for d in FAR_FIRST:
                send(own, err_far.at[q, z - 3], ef_send.at[q], ef_recv.at[q], across_z(d))

    spreads = [
        Spread(
            err.at[q],
            lambda b, i, q=q: err.at[q, b, pl.ds(4 * i, 4)],
            keep,
            1 - keep,
            ep_send.at[q],
            lambda slot, q=q: ep_recv.at[q, slot],
        )
        for q in range(NQ)
    ]

    def z_spread(q):
        wait(err.at[q, 0, pl.ds(0, 7)], ez_recv.at[q])
        wait(err_far.at[q], ef_recv.at[q])
        wait(err.at[q, 0, pl.ds(0, 7)], ez_send.at[q])

        @pl.when(z >= 3)
        def _():
            wait(err.at[q, 0], ef_send.at[q])

        for zz in range(3, NZ):
            far = err_far[q, zz - 3].astype(F32)
            if q == 2 and zz == 4:
                lane = lax.broadcasted_iota(jnp.int32, (ROWS, WIDE), 1)
                far = jnp.where(lane < LANES, 0.0, far)
            err[q, g_keep, zz] = (err[q, g_keep, zz].astype(F32) + far).astype(BF16)
        spreads[q].start()

    def arrived(q):
        spreads[q].finish()
        send(err.at[q, :, pl.ds(z_r, 3)], err_sib.at[q, :, pl.ds(0, 3)], es_send.at[q], es_recv.at[q], sibling)
        send(err.at[q, :, pl.ds(3, 2)], err_sib.at[q, :, pl.ds(3, 2)], es_send.at[q], es_recv.at[q], sibling)

    def backward(error, k, tile, count=3):
        where = cols(tile, count)
        dlat_ref[...] += lax.dot_general(
            error, dec[k, :, where], (((1,), (1,)), ((), ())), preferred_element_type=F32
        )
        gdec[k, :, where] = jnp.dot(latt_ref[...], error, preferred_element_type=F32).astype(BF16)

    def whole(value):
        return value.reshape(TOK, value.shape[-1])

    def wide(ref, q, at):
        return jnp.concatenate([whole(ref[q, :, at + i]) for i in range(3)], axis=1)

    def own_back(q):
        backward(wide(err, q, 0), k_a, first_tile(q, 1), 9)
        backward(wide(err, q, 5), k_b, first_tile(q, 0), 9)

        backward(whole(err[q, :, MID]), k_c, own + 3 * q)
        if q == 0:
            backward(whole(err[q, :, MID + 1]), k_c, own + 9)
        elif q == 1:
            backward(whole(err[q, :, MID + 1, :, 0 : 2 * LANES]), k_c, own + 12, 2)
        else:
            backward(whole(err[q, :, MID + 1, :, 0:LANES]), k_a, 27, 1)
            backward(whole(err[q, :, MID + 1, :, LANES : 2 * LANES]), k_b, 0, 1)

    def sibling_back(q):
        wait(err_sib.at[q], es_recv.at[q])

        backward(wide(err_sib, q, 0), k_s, first_tile(q, send_a), 9)

        backward(whole(err_sib[q, :, 3]), k_c, other + 3 * q)
        if q == 0:
            backward(whole(err_sib[q, :, 4]), k_c, other + 9)
        elif q == 1:
            backward(whole(err_sib[q, :, 4, :, 0 : 2 * LANES]), k_c, other + 12, 2)
        else:
            lanes = pl.ds(pl.multiple_of((1 - send_a) * LANES, LANES), LANES)
            backward(whole(err_sib[q, :, 4, :, lanes]), k_s, 27 * send_a, 1)

    for_sibling(0)
    own_alone(0)
    for_sibling(1)
    own_shared(0)
    y_first(0)
    own_alone(1)
    for_sibling(2)
    own_shared(1)
    y_first(1)
    own_alone(2)
    y_second(0)
    own_shared(2)
    y_first(2)
    y_second(1)
    y_sum(0)
    y_second(2)
    y_sum(1)
    for c in range(TILES):
        block = xb[:, c // 14, :, (c % 14) * LANES : (c % 14 + 1) * LANES].reshape(TOK, LANES)
        xt[c * LANES : (c + 1) * LANES, :] = block.T
    dlat_ref[...] = jnp.zeros_like(dlat_ref)
    z_sum(0)
    y_sum(2)
    z_sum(1)
    z_spread(0)
    z_sum(2)
    z_spread(1)
    spreads[0].second()
    spreads[0].third()
    z_spread(2)
    spreads[1].second()
    arrived(0)
    spreads[1].third()
    own_back(0)
    spreads[2].second()
    spreads[2].third()
    arrived(1)
    sibling_back(0)
    own_back(1)
    sibling_back(1)
    arrived(2)
    own_back(2)
    sibling_back(2)

    wait(xz.at[pl.ds(0, 7)], xz_send)
    x_spread.left_here()
    for q in range(NQ):
        wait(sib_in.at[q], sib_send.at[q])
        wait(y_in.at[q], y_send.at[q])
        wait(z_in.at[q], z_send.at[q])
        spreads[q].left_here()
        wait(err_sib.at[q], es_send.at[q])


def last_kernel(gdec, xt, mask, dlat, genc_hbm, gdec_hbm, genc, sem):
    gdec_copy = pltpu.make_async_copy(gdec, gdec_hbm.at[0], sem.at[0])
    gdec_copy.start()
    dpre = (mask[...] * dlat[...]).astype(BF16)
    genc[...] = jnp.dot(xt[...], dpre, preferred_element_type=F32).astype(BF16)
    genc_copy = pltpu.make_async_copy(genc, genc_hbm.at[0], sem.at[1])
    genc_copy.start()
    gdec_copy.wait()
    genc_copy.wait()


def local(inputs, encoder, active, decoder, goals):
    vmem = pl.BlockSpec(memory_space=pltpu.VMEM)
    hbm = pl.BlockSpec(memory_space=pl.ANY)
    dma = pltpu.SemaphoreType.DMA
    per_q = [dma((NQ,))] * 2
    gdec, xt, mask, dlat = pl.pallas_call(
        kernel,
        out_shape=(
            pltpu.VMEM((4, FL, D), BF16),
            pltpu.VMEM((D, TOK), BF16),
            pltpu.VMEM((TOK, FL), F32),
            pltpu.VMEM((TOK, FL), F32),
        ),
        in_specs=[pl.BlockSpec(memory_space=pltpu.HBM)] * 5,
        out_specs=[vmem] * 4,
        scratch_shapes=[
            pltpu.VMEM((2, D), BF16),
            pltpu.VMEM((7, 2, D), BF16),
            pltpu.VMEM((TOK, FL), jnp.int32),
            pltpu.VMEM((D, FL), BF16),
            pltpu.VMEM((4, FL, D), BF16),
            pltpu.VMEM((XROWS, LANES), F32),
            pltpu.VMEM((NZ, XROWS, LANES), BF16),
            pltpu.VMEM((NZ * XROWS, LANES), F32),
            pltpu.VMEM((NG, 2, ROWS, D // 2), BF16),
            pltpu.VMEM((TOK, FL), BF16),
            pltpu.VMEM((FL, TOK), BF16),
            pltpu.VMEM((NQ, NZ, ROWS, WIDE), F32),
            pltpu.VMEM((NQ, 5, NG, ROWS, WIDE), BF16),
            pltpu.VMEM((NQ, 5, NG, ROWS, WIDE), BF16),
            pltpu.VMEM((NQ, NG, NZ, ROWS, WIDE), BF16),
            pltpu.VMEM((NQ, 6, NZ, ROWS, WIDE), BF16),
            pltpu.VMEM((NQ, 15, ROWS, WIDE), BF16),
            pltpu.VMEM((NQ, NG, NZ, ROWS, WIDE), BF16),
            pltpu.VMEM((NQ, 5, ROWS, WIDE), BF16),
            pltpu.VMEM((NQ, NG, 5, ROWS, WIDE), BF16),
            dma((5,)),
            dma,
            dma,
            dma,
            dma((9,)),
            *per_q,
            dma((NQ,)),
            dma((NQ, 3)),
            *per_q,
            *per_q,
            *per_q,
            dma((NQ,)),
            dma((NQ, 9)),
            *per_q,
        ],
        compiler_params=pltpu.CompilerParams(
            collective_id=0, has_side_effects=True, vmem_limit_bytes=54 * 2**20
        ),
        name="step",
    )(inputs, goals, active, encoder, decoder)
    return pl.pallas_call(
        last_kernel,
        out_shape=(
            jax.ShapeDtypeStruct((1, D, FL), BF16),
            jax.ShapeDtypeStruct((1, 4, FL, D), BF16),
        ),
        in_specs=[vmem] * 4,
        out_specs=(hbm, hbm),
        scratch_shapes=[pltpu.VMEM((D, FL), BF16), dma((2,))],
        compiler_params=pltpu.CompilerParams(vmem_limit_bytes=8 * 2**20),
        name="write",
    )(gdec, xt, mask, dlat)


def solution(mesh):
    return jax.shard_map(
        local,
        mesh=mesh,
        in_specs=(
            P("layer", "slab", None),
            P("layer", None, "slab"),
            P("layer", None, "slab"),
            P("layer", None, "slab", None),
            P(None, "slab", None),
        ),
        out_specs=(P("layer", None, "slab"), P("layer", None, "slab", None)),
        check_vma=False,
    )
```

```python
import math

import jax
import jax.numpy as jnp
from jax import lax
from jax.experimental import pallas as pl
from jax.experimental.pallas import tpu as pltpu
from jax.sharding import PartitionSpec as P

MESH = pl.DeviceIdType.MESH
F32, BF16 = jnp.float32, jnp.bfloat16

NZ, NG = 8, 8
TOK, D, FL = 128, 3584, 128
ROWS = 16
LANES = 128
TILES = D // LANES
NQ = 3
TILES_OF = (4, 3, 2)
FIRST = (0, 4, 7)
XROWS = 64
MID = 3
FAR_FIRST = (4, 3, 5, 2, 6, 1, 7, 0)


def cols(tile, count=3):
    return pl.ds(pl.multiple_of(tile * LANES, LANES), count * LANES)


def kernel(
    inputs_hbm,
    goals_hbm,
    active_hbm,
    enc_hbm,
    dec_hbm,
    gdec,
    xt,
    mask,
    dlat_ref,
    inputs_ref,
    goals_ref,
    active_ref,
    enc,
    dec,
    xstage,
    xz,
    xwide,
    xb,
    lat_ref,
    latt_ref,
    goal_block,
    sib_out,
    sib_in,
    part,
    y_in,
    half_in,
    pair_in,
    x_in,
    z_in,
    bulk_in,
    plane_in,
    term,
    err,
    err_far,
    plane_far,
    err_sib,
    load_sem,
    xz_send,
    xz_recv,
    xb_send,
    xb_recv,
    sib_send,
    sib_recv,
    y_send,
    y_recv,
    x_send,
    x_recv,
    pair_recv,
    z_send,
    z_recv,
    ez_send,
    ez_recv,
    ef_send,
    ef_recv,
    ep_send,
    ep_recv,
    es_send,
    es_recv,
    bulk_send,
    bulk_recv,
    plane_send,
    plane_recv,
    far_send,
    far_recv,
):
    layer = lax.axis_index("layer")
    slab = lax.axis_index("slab")
    x_hi, core = layer // 2, layer % 2
    z, g = slab // NG, slab % NG
    y, x = g // 2, g % 2
    y1, y2, y3 = (y + 1) % 4, (y + 2) % 4, (y + 3) % 4
    keep = (x + x_hi) % 2
    g_keep, g_pass = y * 2 + keep, y * 2 + 1 - keep
    scale = 1.0 / math.sqrt(TOK)

    def z_peer(d):
        return (layer, ((z + d) % NZ) * NG + g)

    def plane_peer(d):
        return (layer, z * NG + (g + d) % NG)

    def across_plane(d):
        return ((1 - x_hi) * 2 + core, z * NG + (g + d) % NG)

    def across_z(d):
        return ((1 - x_hi) * 2 + core, ((z + d) % NZ) * NG + y * 2 + 1 - x)

    right = (layer, z * NG + y1 * 2 + x)
    left = (layer, z * NG + y3 * 2 + x)
    pair = (layer, z * NG + y * 2 + 1 - x)
    sibling = (x_hi * 2 + 1 - core, slab)
    right_pair = (layer, z * NG + y1 * 2 + 1 - x)
    left_pair = (layer, z * NG + y3 * 2 + 1 - x)

    k_a = 3 * x_hi
    k_b = (layer + 2) % 4
    k_c = 3 - layer
    k_s = 1 + x_hi
    send_a = (core + x_hi + 1) % 2
    recv_a = 1 - send_a
    k_r = recv_a * k_a + (1 - recv_a) * k_b
    k_n = (1 - recv_a) * k_a + recv_a * k_b
    z_s, z_r, z_n = 5 * (1 - send_a), 5 * (1 - recv_a), 5 * recv_a

    def first_tile(q, is_a):
        return 3 * FIRST[q] + 1 - is_a

    loads = [
        pltpu.make_async_copy(src, dst, load_sem.at[i])
        for i, (src, dst) in enumerate(
            [
                (inputs_hbm.at[0], inputs_ref),
                (active_hbm.at[0], active_ref),
                (goals_hbm, goals_ref),
                (enc_hbm.at[0], enc),
                (dec_hbm.at[0], dec),
            ]
        )
    ]
    for load in loads:
        load.start()

    barrier = pltpu.get_barrier_semaphore()

    def greet(device):
        pl.semaphore_signal(barrier, inc=1, device_id=device, device_id_type=MESH)

    for d in FAR_FIRST:
        greet(across_z(d))
        greet(across_plane(d))
        if d:
            greet(z_peer(d))
            greet(plane_peer(d))
    greet(sibling)

    xstage[...] = jnp.zeros_like(xstage)
    loads[0].wait()
    for c in range(TILES):
        xstage[2 * c : 2 * c + 2, :] = inputs_ref[:, c * LANES : (c + 1) * LANES].astype(F32)
    xz[z] = xstage[...].astype(BF16)

    pl.semaphore_wait(barrier, 31)

    def send(src, dst, ssem, rsem, device):
        pltpu.make_async_remote_copy(
            src_ref=src, dst_ref=dst, send_sem=ssem, recv_sem=rsem, device_id=device, device_id_type=MESH
        ).start()

    def wait(ref, sem):
        pltpu.make_async_copy(ref, ref, sem).wait()

    class Spread:
        def __init__(self, buf, half, near, mate, ssem, rsem, direct):
            self.buf, self.half, self.near, self.mate = buf, half, near, mate
            self.direct = direct
            self.ssem, self.rsem = ssem, rsem

        def put(self, block, slot, device):
            send(self.buf.at[block], self.buf.at[block], self.ssem, self.rsem(slot), device)

        def put_half(self, block, i, slot, device):
            part_of = self.half(block, i)
            send(part_of, part_of, self.ssem, self.rsem(slot), device)

        def got(self, slot):
            wait(self.buf.at[0], self.rsem(slot))

        def start(self):
            own = y * 2 + self.near
            self.put(own, 1, right)
            self.put(own, 2, left)
            if self.direct:
                self.put(own, 3, right_pair)
                self.put(own, 4, left_pair)
            self.put(own, 0, pair)

        def from_pair(self):
            self.got(0)
            self.put(y * 2 + self.mate, 3, right)
            self.put(y * 2 + self.mate, 4, left)

        def onward(self, which, slot):
            self.got(slot)
            self.put_half(y3 * 2 + which, 0, slot + 4, right)
            self.got(slot + 1)
            self.put_half(y1 * 2 + which, 1, slot + 5, left)

        def second(self):
            self.onward(self.near, 1)

        def third(self):
            self.onward(self.mate, 3)

        def finish(self):
            if self.direct:
                self.got(0)
            for slot in range(5, 9):
                wait(self.half(0, 0), self.rsem(slot))

        def left_here(self):
            wait(self.buf.at[pl.ds(0, 7)], self.ssem)

    for d in FAR_FIRST[:7]:
        send(xz.at[z], xz.at[z], xz_send, xz_recv, z_peer(d))

    loads[1].wait()
    for gg in range(NG):
        for r in range(2):
            mask[gg * ROWS + r * 8 : gg * ROWS + r * 8 + 8, :] = active_ref[
                pl.ds(gg * 2 + r, 8, stride=16), :
            ].astype(F32)

    mine = lax.broadcasted_iota(jnp.int32, (8, 1), 0) == z
    loads[2].wait()

    first_half = (1 - x_hi).astype(F32)

    def goal_rows(target, tile, count, factor=first_half):
        two = goals_ref[target, :, cols(tile, count)].astype(F32) * factor
        zero = jnp.zeros((8, count * LANES), F32)
        return jnp.concatenate([jnp.where(mine, two[r : r + 1], zero) for r in range(2)], axis=0)

    t_a, t_b = 5 * x_hi + core, 2 + 2 * core
    for q, w in enumerate(TILES_OF):
        for zz in range(3):
            goal_block[q][zz] = goal_rows(t_a, 3 * FIRST[q] + w * zz, w, 1.0)
            goal_block[q][zz + 5] = goal_rows(t_b, 3 * FIRST[q] + 1 + w * zz, w)
        goal_block[q][MID] = goal_rows(3, core * 14 + FIRST[q], w)
    goal_block[0][MID + 1] = goal_rows(3, core * 14 + 9, 4)
    goal_block[1][MID + 1, :, 0:LANES] = goal_rows(3, core * 14 + 13, 1)
    goal_block[1][MID + 1, :, LANES : 2 * LANES] = goal_rows(t_a, 27, 1, 1.0)
    goal_block[1][MID + 1, :, 2 * LANES :] = goal_rows(t_b, 0, 1)
    goal_block[2][MID + 1] = jnp.zeros((ROWS, 2 * LANES), F32)

    wait(xz.at[pl.ds(0, 7)], xz_recv)
    for zz in range(NZ):
        xwide[zz * XROWS : (zz + 1) * XROWS, :] = xz[zz].astype(F32)
    for c in range(TILES):
        xb[g, c // 14, :, (c % 14) * LANES : (c % 14 + 1) * LANES] = jnp.concatenate(
            [xwide[pl.ds(2 * c + r, 8, stride=XROWS), :] for r in range(2)], axis=0
        ).astype(BF16)

    x_spread = Spread(xb, lambda b, i: xb.at[b, i], x, 1 - x, xb_send, lambda slot: xb_recv.at[slot], True)
    x_spread.start()
    x_spread.second()
    x_spread.third()
    loads[3].wait()
    loads[4].wait()
    x_spread.finish()

    pre = jnp.dot(xb[:, 0].reshape(TOK, D // 2), enc[: D // 2, :], preferred_element_type=F32)
    pre = pre + jnp.dot(xb[:, 1].reshape(TOK, D // 2), enc[D // 2 :, :], preferred_element_type=F32)
    act = mask[...] * pre
    lat_ref[...] = act.astype(BF16)
    latt_ref[...] = act.T.astype(BF16)

    def decoded(k, tile, count=3):
        return jnp.dot(lat_ref[...], dec[k, :, cols(tile, count)], preferred_element_type=F32)

    def blocks(value):
        return value.reshape(NG, ROWS, value.shape[-1])

    other = (1 - core) * 14
    own = core * 14
    is_a, is_b = send_a.astype(F32), (1 - send_a).astype(F32)
    empty = jnp.zeros((NG, ROWS, 2 * LANES), BF16)

    def cut(value, q, i):
        w = TILES_OF[q] * LANES
        return blocks(value[:, i * w : (i + 1) * w])

    def for_sibling(q):
        w = TILES_OF[q]
        wide = decoded(k_s, first_tile(q, send_a), 3 * w).astype(BF16)
        for i in range(3):
            sib_out[q][i] = cut(wide, q, i)
        sib_out[q][3] = blocks(decoded(k_c, other + FIRST[q], w).astype(BF16))
        if q == 0:
            sib_out[q][4] = blocks(decoded(k_c, other + 9, 4).astype(BF16))
        elif q == 1:
            sib_out[q][4, :, :, 0:LANES] = blocks(decoded(k_c, other + 13, 1).astype(BF16))
            sib_out[q][4, :, :, LANES : 2 * LANES] = blocks((decoded(k_s, 27, 1) * is_a).astype(BF16))
            sib_out[q][4, :, :, 2 * LANES :] = blocks((decoded(k_s, 0, 1) * is_b).astype(BF16))
        else:
            sib_out[q][4] = empty
        send(sib_out[q], sib_in[q], sib_send.at[q], sib_recv.at[q], sibling)

    def own_alone(q):
        wide = decoded(k_n, first_tile(q, 1 - recv_a), 3 * TILES_OF[q]).astype(BF16)
        for i in range(3):
            part[q][:, z_n + i] = cut(wide, q, i)

    def own_shared(q):
        wait(sib_in[q], sib_recv.at[q])
        w = TILES_OF[q]
        wide = decoded(k_r, first_tile(q, recv_a), 3 * w)
        for i in range(3):
            part[q][:, z_r + i] = (cut(wide, q, i) + sib_in[q][i].astype(F32)).astype(BF16)
        part[q][:, MID] = (blocks(decoded(k_c, own + FIRST[q], w)) + sib_in[q][3].astype(F32)).astype(BF16)

        def last(lanes, value):
            part[q][:, MID + 1, :, lanes] = (blocks(value) + sib_in[q][4, :, :, lanes].astype(F32)).astype(BF16)

        if q == 0:
            last(slice(0, 4 * LANES), decoded(k_c, own + 9, 4))
        elif q == 1:
            last(slice(0, LANES), decoded(k_c, own + 13, 1))
            last(slice(LANES, 2 * LANES), decoded(k_a, 27, 1))
            last(slice(2 * LANES, 3 * LANES), decoded(k_b, 0, 1))
        else:
            part[q][:, MID + 1] = empty

    def less_goals(q):
        for zz in range(NZ):
            part[q][g, zz] = (part[q][g, zz].astype(F32) - goal_block[q][zz]).astype(BF16)

    def y_first(q):
        ss = y_send.at[0]
        send(part[q].at[y2 * 2], y_in.at[0], ss, y_recv.at[0, 0], right)
        send(part[q].at[y2 * 2 + 1], y_in.at[1], ss, y_recv.at[0, 1], left)
        send(part[q].at[y1 * 2 + 1], y_in.at[2], ss, y_recv.at[0, 2], right)
        send(part[q].at[y3 * 2], y_in.at[3], ss, y_recv.at[0, 2], left)

    def y_second(q):
        ss = y_send.at[0]
        wait(y_in.at[0], y_recv.at[0, 0])
        for zz in range(NZ):
            part[q][y1 * 2, zz] = (part[q][y1 * 2, zz].astype(F32) + y_in[0, zz].astype(F32)).astype(BF16)
        send(part[q].at[y1 * 2], y_in.at[4], ss, y_recv.at[0, 2], right)
        wait(y_in.at[1], y_recv.at[0, 1])
        for zz in range(NZ):
            part[q][y3 * 2 + 1, zz] = (
                part[q][y3 * 2 + 1, zz].astype(F32) + y_in[1, zz].astype(F32)
            ).astype(BF16)
        send(part[q].at[y3 * 2 + 1], y_in.at[5], ss, y_recv.at[0, 2], left)

    def y_sum(q):
        wait(y_in.at[pl.ds(0, 4)], y_recv.at[0, 2])
        for half, (one, two) in enumerate(((3, 4), (2, 5))):
            here = (x == half).astype(F32)
            for zz in range(NZ):
                part[q][y * 2 + half, zz] = (
                    part[q][y * 2 + half, zz].astype(F32)
                    + y_in[one, zz].astype(F32)
                    + y_in[two, zz].astype(F32)
                    - goal_block[q][zz] * here
                ).astype(BF16)
        send(part[q].at[g_pass], x_in, x_send.at[0], x_recv.at[0], pair)

    def to_z(q):
        for d in FAR_FIRST[:7]:
            send(part[q].at[g_keep, (z + d) % NZ], z_in[q].at[d - 1], z_send.at[q], z_recv.at[q], z_peer(d))

    def x_sum(q):
        wait(x_in, x_recv.at[0])
        for zz in range(NZ):
            part[q][g_keep, zz] = (part[q][g_keep, zz].astype(F32) + x_in[zz].astype(F32)).astype(BF16)
        to_z(q)

    def pair_first():
        less_goals(1)
        for j in (2, 1, 3, 0):
            send(
                part[1].at[((y + j) % 4) * 2 + 1 - keep], pair_in.at[j], x_send.at[1], pair_recv.at[j], pair
            )

    def pair_sum(j):
        wait(pair_in.at[j], pair_recv.at[j])
        to = ((y + j) % 4) * 2 + keep
        for zz in range(NZ):
            part[1][to, zz] = (part[1][to, zz].astype(F32) + pair_in[j, zz].astype(F32)).astype(BF16)

    low, high = pl.ds(0, 4), pl.ds(4, 4)

    def half_first():
        ss = y_send.at[1]
        pair_sum(2)
        send(part[1].at[y2 * 2 + keep, low], half_in.at[0], ss, y_recv.at[1, 0], right)
        send(part[1].at[y2 * 2 + keep, high], half_in.at[1], ss, y_recv.at[1, 1], left)
        pair_sum(1)
        send(part[1].at[y1 * 2 + keep, high], half_in.at[2], ss, y_recv.at[1, 2], right)
        pair_sum(3)
        send(part[1].at[y3 * 2 + keep, low], half_in.at[3], ss, y_recv.at[1, 2], left)
        pair_sum(0)

    def half_second():
        ss = y_send.at[1]
        wait(half_in.at[0], y_recv.at[1, 0])
        to = y1 * 2 + keep
        for zz in range(4):
            part[1][to, zz] = (part[1][to, zz].astype(F32) + half_in[0, zz].astype(F32)).astype(BF16)
        send(part[1].at[to, low], half_in.at[4], ss, y_recv.at[1, 2], right)
        wait(half_in.at[1], y_recv.at[1, 1])
        to = y3 * 2 + keep
        for zz in range(4):
            part[1][to, zz + 4] = (part[1][to, zz + 4].astype(F32) + half_in[1, zz].astype(F32)).astype(BF16)
        send(part[1].at[to, high], half_in.at[5], ss, y_recv.at[1, 2], left)

    def half_sum():
        wait(half_in.at[pl.ds(0, 4)], y_recv.at[1, 2])
        for at, one, two in ((0, 3, 4), (4, 2, 5)):
            for zz in range(4):
                part[1][g_keep, at + zz] = (
                    part[1][g_keep, at + zz].astype(F32)
                    + half_in[one, zz].astype(F32)
                    + half_in[two, zz].astype(F32)
                ).astype(BF16)
        to_z(1)

    def z_sum(q):
        wait(z_in[q], z_recv.at[q])
        total = part[q][g_keep, z].astype(F32)
        for i in range(7):
            total = total + z_in[q][i].astype(F32)
        value = (total * scale).astype(BF16)
        term[q][...] = value
        err[q][g_keep, z] = value
        own = term[q]
        for d in FAR_FIRST[:7]:
            send(own, err[q].at[g_keep, z], ez_send.at[q], ez_recv.at[q], z_peer(d))

        @pl.when(z >= 3)
        def _():
            for d in FAR_FIRST:
                send(own, err_far[q].at[z - 3], ef_send.at[q], ef_recv.at[q], across_z(d))

    def bulk_first():
        less_goals(2)
        for d in FAR_FIRST[:7]:
            send(part[2].at[:, (z + d) % NZ], bulk_in.at[d - 1], bulk_send.at[0], bulk_recv.at[0], z_peer(d))

    def bulk_sum():
        wait(bulk_in, bulk_recv.at[0])
        for gg in range(NG):
            total = part[2][gg, z].astype(F32)
            for i in range(7):
                total = total + bulk_in[i, gg].astype(F32)
            part[2][gg, z] = total.astype(BF16)
        for d in range(1, 8):
            send(
                part[2].at[(g + d) % NG, z], plane_in.at[d - 1], plane_send.at[0], plane_recv.at[0], plane_peer(d)
            )

    def plane_sum():
        wait(plane_in, plane_recv.at[0])
        total = part[2][g, z].astype(F32)
        for i in range(7):
            total = total + plane_in[i].astype(F32)
        value = (total * scale).astype(BF16)
        term[2][...] = value
        err[2][g, z] = value
        own = term[2]
        for d in range(1, 8):
            send(own, err[2].at[g, z], plane_send.at[1], plane_recv.at[1], plane_peer(d))

        @pl.when(z >= 3)
        def _():
            for d in FAR_FIRST:
                send(own, plane_far.at[g], far_send, far_recv, across_plane(d))

    def plane_spread():
        wait(plane_in, plane_recv.at[1])

        @pl.when(z >= 3)
        def _():
            wait(plane_far, far_recv)
            for gg in range(NG):
                err[2][gg, z] = (err[2][gg, z].astype(F32) + plane_far[gg].astype(F32)).astype(BF16)

        for d in FAR_FIRST[:7]:
            send(err[2].at[:, z], err[2].at[:, z], bulk_send.at[1], bulk_recv.at[1], z_peer(d))

    def to_sibling(q):
        send(err[q].at[:, pl.ds(z_r, 3)], err_sib[q].at[:, pl.ds(0, 3)], es_send.at[q], es_recv.at[q], sibling)
        send(err[q].at[:, pl.ds(3, 2)], err_sib[q].at[:, pl.ds(3, 2)], es_send.at[q], es_recv.at[q], sibling)

    def bulk_arrived():
        wait(bulk_in, bulk_recv.at[1])
        to_sibling(2)

    y_spread = Spread(
        err[0],
        lambda b, i: err[0].at[b, pl.ds(4 * i, 4)],
        keep,
        1 - keep,
        ep_send.at[0],
        lambda slot: ep_recv.at[0, slot],
        False,
    )

    class HalfSpread:
        def put(self, block, which, slot, device):
            at = err[1].at[block] if which is None else err[1].at[block, which]
            send(at, at, ep_send.at[1], ep_recv.at[1, slot], device)

        def got(self, slot, which=None):
            wait(err[1].at[0] if which is None else err[1].at[0, which], ep_recv.at[1, slot])

        def start(self):
            self.put(g_keep, None, 0, right)
            self.put(g_keep, None, 1, left)
            self.put(g_keep, None, 4, pair)

        def second(self):
            self.got(0)
            self.put(y3 * 2 + keep, low, 2, right)
            self.put(y3 * 2 + keep, None, 5, pair)
            self.got(1)
            self.put(y1 * 2 + keep, high, 3, left)
            self.put(y1 * 2 + keep, None, 6, pair)

        def third(self):
            self.got(2, low)
            self.put(y2 * 2 + keep, low, 7, pair)
            self.got(3, high)
            self.put(y2 * 2 + keep, high, 8, pair)

        def finish(self):
            for slot in (4, 5, 6):
                self.got(slot)
            self.got(7, low)
            self.got(8, high)

        def left_here(self):
            wait(err[1].at[pl.ds(0, 7)], ep_send.at[1])

    spreads = [y_spread, HalfSpread()]

    def z_spread(q):
        wait(err[q].at[0, pl.ds(0, 7)], ez_recv.at[q])
        wait(err_far[q], ef_recv.at[q])
        for zz in range(3, NZ):
            far = err_far[q][zz - 3].astype(F32)
            if q == 1 and zz == 4:
                tile = lax.broadcasted_iota(jnp.int32, (ROWS, 3 * LANES), 1) // LANES
                far = jnp.where(tile == 1, 0.0, far)
            err[q][g_keep, zz] = (err[q][g_keep, zz].astype(F32) + far).astype(BF16)
        spreads[q].start()

    def arrived(q):
        spreads[q].finish()
        to_sibling(q)

    def backward(error, k, tile, count=3):
        where = cols(tile, count)
        dlat_ref[...] += lax.dot_general(
            error, dec[k, :, where], (((1,), (1,)), ((), ())), preferred_element_type=F32
        )
        gdec[k, :, where] = jnp.dot(latt_ref[...], error, preferred_element_type=F32).astype(BF16)

    def whole(value):
        return value.reshape(TOK, value.shape[-1])

    def wide(ref, q, at):
        return jnp.concatenate([whole(ref[q][:, at + i]) for i in range(3)], axis=1)

    def own_back(q):
        w = TILES_OF[q]
        backward(wide(err, q, 0), k_a, first_tile(q, 1), 3 * w)
        backward(wide(err, q, 5), k_b, first_tile(q, 0), 3 * w)
        backward(whole(err[q][:, MID]), k_c, own + FIRST[q], w)
        if q == 0:
            backward(whole(err[q][:, MID + 1]), k_c, own + 9, 4)
        elif q == 1:
            backward(whole(err[q][:, MID + 1, :, 0:LANES]), k_c, own + 13, 1)
            backward(whole(err[q][:, MID + 1, :, LANES : 2 * LANES]), k_a, 27, 1)
            backward(whole(err[q][:, MID + 1, :, 2 * LANES :]), k_b, 0, 1)

    def sibling_back(q):
        wait(err_sib[q], es_recv.at[q])
        w = TILES_OF[q]
        backward(wide(err_sib, q, 0), k_s, first_tile(q, send_a), 3 * w)
        backward(whole(err_sib[q][:, 3]), k_c, other + FIRST[q], w)
        if q == 0:
            backward(whole(err_sib[q][:, 4]), k_c, other + 9, 4)
        elif q == 1:
            backward(whole(err_sib[q][:, 4, :, 0:LANES]), k_c, other + 13, 1)
            lanes = pl.ds(pl.multiple_of((2 - send_a) * LANES, LANES), LANES)
            backward(whole(err_sib[q][:, 4, :, lanes]), k_s, 27 * send_a, 1)

    for_sibling(1)
    for_sibling(0)
    own_alone(1)
    own_shared(1)
    pair_first()
    for_sibling(2)
    own_alone(0)
    own_shared(0)
    y_first(0)
    own_alone(2)
    own_shared(2)
    bulk_first()
    y_second(0)
    half_first()
    half_second()
    y_sum(0)
    half_sum()
    x_sum(0)
    for c in range(TILES):
        block = xb[:, c // 14, :, (c % 14) * LANES : (c % 14 + 1) * LANES].reshape(TOK, LANES)
        xt[c * LANES : (c + 1) * LANES, :] = block.T
    dlat_ref[...] = jnp.zeros_like(dlat_ref)
    bulk_sum()
    z_sum(1)
    plane_sum()
    z_sum(0)
    plane_spread()
    z_spread(1)
    z_spread(0)
    spreads[1].second()
    spreads[0].from_pair()
    spreads[1].third()
    spreads[0].second()
    spreads[0].third()
    arrived(1)
    bulk_arrived()
    own_back(1)
    own_back(2)
    sibling_back(1)
    arrived(0)
    own_back(0)
    sibling_back(2)
    sibling_back(0)

    wait(xz.at[pl.ds(0, 7)], xz_send)
    x_spread.left_here()
    for q in range(NQ):
        wait(sib_in[q], sib_send.at[q])
        wait(err_sib[q], es_send.at[q])
    for q in range(2):
        wait(z_in[q], z_send.at[q])
        wait(z_in[q], ez_send.at[q])
        spreads[q].left_here()
    wait(y_in, y_send.at[0])
    wait(half_in, y_send.at[1])
    wait(x_in, x_send.at[0])
    wait(pair_in, x_send.at[1])
    for i in range(2):
        wait(bulk_in, bulk_send.at[i])
        wait(plane_in, plane_send.at[i])

    @pl.when(z >= 3)
    def _():
        for q in range(2):
            wait(err[q].at[0], ef_send.at[q])
        wait(plane_far, far_send)


def last_kernel(gdec, xt, mask, dlat, genc_hbm, gdec_hbm, genc, sem):
    gdec_copy = pltpu.make_async_copy(gdec, gdec_hbm.at[0], sem.at[0])
    gdec_copy.start()
    dpre = (mask[...] * dlat[...]).astype(BF16)
    genc[...] = jnp.dot(xt[...], dpre, preferred_element_type=F32).astype(BF16)
    genc_copy = pltpu.make_async_copy(genc, genc_hbm.at[0], sem.at[1])
    genc_copy.start()
    gdec_copy.wait()
    genc_copy.wait()


def local(inputs, encoder, active, decoder, goals):
    vmem = pl.BlockSpec(memory_space=pltpu.VMEM)
    hbm = pl.BlockSpec(memory_space=pl.ANY)
    dma = pltpu.SemaphoreType.DMA
    per_q = [dma((NQ,))] * 2

    def chunk(q, shape, dtype=BF16):
        return pltpu.VMEM((*shape, TILES_OF[q] * LANES), dtype)

    def chunks(shape, dtype=BF16):
        return [chunk(q, shape, dtype) for q in range(NQ)]

    gdec, xt, mask, dlat = pl.pallas_call(
        kernel,
        out_shape=(
            pltpu.VMEM((4, FL, D), BF16),
            pltpu.VMEM((D, TOK), BF16),
            pltpu.VMEM((TOK, FL), F32),
            pltpu.VMEM((TOK, FL), F32),
        ),
        in_specs=[pl.BlockSpec(memory_space=pltpu.HBM)] * 5,
        out_specs=[vmem] * 4,
        scratch_shapes=[
            pltpu.VMEM((2, D), BF16),
            pltpu.VMEM((7, 2, D), BF16),
            pltpu.VMEM((TOK, FL), jnp.int32),
            pltpu.VMEM((D, FL), BF16),
            pltpu.VMEM((4, FL, D), BF16),
            pltpu.VMEM((XROWS, LANES), F32),
            pltpu.VMEM((NZ, XROWS, LANES), BF16),
            pltpu.VMEM((NZ * XROWS, LANES), F32),
            pltpu.VMEM((NG, 2, ROWS, D // 2), BF16),
            pltpu.VMEM((TOK, FL), BF16),
            pltpu.VMEM((FL, TOK), BF16),
            chunks((NZ, ROWS), F32),
            chunks((5, NG, ROWS)),
            chunks((5, NG, ROWS)),
            chunks((NG, NZ, ROWS)),
            chunk(0, (6, NZ, ROWS)),
            chunk(1, (6, 4, ROWS)),
            chunk(1, (4, NZ, ROWS)),
            chunk(0, (NZ, ROWS)),
            chunks((NZ - 1, ROWS))[:2],
            chunk(2, (NZ - 1, NG, ROWS)),
            chunk(2, (NG - 1, ROWS)),
            chunks((ROWS,)),
            chunks((NG, NZ, ROWS)),
            chunks((5, ROWS))[:2],
            chunk(2, (NG, ROWS)),
            chunks((NG, 5, ROWS)),
            dma((5,)),
            dma,
            dma,
            dma,
            dma((9,)),
            *per_q,
            dma((NQ,)),
            dma((NQ, 3)),
            *per_q,
            dma((4,)),
            *per_q,
            *per_q,
            *per_q,
            dma((NQ,)),
            dma((NQ, 9)),
            *per_q,
            dma((2,)),
            dma((2,)),
            dma((2,)),
            dma((2,)),
            dma,
            dma,
        ],
        compiler_params=pltpu.CompilerParams(
            collective_id=0, has_side_effects=True, vmem_limit_bytes=54 * 2**20
        ),
        name="step",
    )(inputs, goals, active, encoder, decoder)
    return pl.pallas_call(
        last_kernel,
        out_shape=(
            jax.ShapeDtypeStruct((1, D, FL), BF16),
            jax.ShapeDtypeStruct((1, 4, FL, D), BF16),
        ),
        in_specs=[vmem] * 4,
        out_specs=(hbm, hbm),
        scratch_shapes=[pltpu.VMEM((D, FL), BF16), dma((2,))],
        compiler_params=pltpu.CompilerParams(vmem_limit_bytes=8 * 2**20),
        name="write",
    )(gdec, xt, mask, dlat)


def solution(mesh):
    return jax.shard_map(
        local,
        mesh=mesh,
        in_specs=(
            P("layer", "slab", None),
            P("layer", None, "slab"),
            P("layer", None, "slab"),
            P("layer", None, "slab", None),
            P(None, "slab", None),
        ),
        out_specs=(P("layer", None, "slab"), P("layer", None, "slab", None)),
        check_vma=False,
    )
```

```python
import math

import jax
import jax.numpy as jnp
from jax import lax
from jax.experimental import pallas as pl
from jax.experimental.pallas import tpu as pltpu
from jax.sharding import PartitionSpec as P

MESH = pl.DeviceIdType.MESH
F32, BF16 = jnp.float32, jnp.bfloat16

NZ, NG = 8, 8
TOK, D, FL = 128, 3584, 128
ROWS = 16
LANES = 128
TILES = D // LANES
NQ = 3
TILES_OF = (4, 3, 2)
FIRST = (0, 4, 7)
XROWS = 64
MID = 3
FAR_FIRST = (4, 3, 5, 2, 6, 1, 7, 0)


def cols(tile, count=3):
    return pl.ds(pl.multiple_of(tile * LANES, LANES), count * LANES)


def kernel(
    inputs_hbm,
    goals_hbm,
    active_hbm,
    enc_hbm,
    dec_hbm,
    gdec,
    xt,
    mask,
    dlat_ref,
    inputs_ref,
    goals_ref,
    active_ref,
    enc,
    dec,
    xstage,
    xz,
    xwide,
    xb,
    lat_ref,
    latt_ref,
    goal_block,
    sib_out,
    sib_in,
    part,
    y_in,
    half_in,
    pair_in,
    x_in,
    z_in,
    bulk_in,
    plane_in,
    term,
    err,
    err_far,
    plane_far,
    err_sib,
    load_sem,
    xz_send,
    xz_recv,
    xb_send,
    xb_recv,
    sib_send,
    sib_recv,
    y_send,
    y_recv,
    x_send,
    x_recv,
    pair_recv,
    z_send,
    z_recv,
    ez_send,
    ez_recv,
    ef_send,
    ef_recv,
    ep_send,
    ep_recv,
    es_send,
    es_recv,
    bulk_send,
    bulk_recv,
    plane_send,
    plane_recv,
    far_send,
    far_recv,
):
    layer = lax.axis_index("layer")
    slab = lax.axis_index("slab")
    x_hi, core = layer // 2, layer % 2
    z, g = slab // NG, slab % NG
    y, x = g // 2, g % 2
    y1, y2, y3 = (y + 1) % 4, (y + 2) % 4, (y + 3) % 4
    keep = (x + x_hi) % 2
    g_keep, g_pass = y * 2 + keep, y * 2 + 1 - keep
    scale = 1.0 / math.sqrt(TOK)

    def z_peer(d):
        return (layer, ((z + d) % NZ) * NG + g)

    def plane_peer(d):
        return (layer, z * NG + (g + d) % NG)

    def across_plane(d):
        return ((1 - x_hi) * 2 + core, z * NG + (g + d) % NG)

    def across_z(d):
        return ((1 - x_hi) * 2 + core, ((z + d) % NZ) * NG + y * 2 + 1 - x)

    right = (layer, z * NG + y1 * 2 + x)
    left = (layer, z * NG + y3 * 2 + x)
    pair = (layer, z * NG + y * 2 + 1 - x)
    sibling = (x_hi * 2 + 1 - core, slab)
    right_pair = (layer, z * NG + y1 * 2 + 1 - x)
    left_pair = (layer, z * NG + y3 * 2 + 1 - x)

    k_a = 3 * x_hi
    k_b = (layer + 2) % 4
    k_c = 3 - layer
    k_s = 1 + x_hi
    send_a = (core + x_hi + 1) % 2
    recv_a = 1 - send_a
    k_r = recv_a * k_a + (1 - recv_a) * k_b
    k_n = (1 - recv_a) * k_a + recv_a * k_b
    z_s, z_r, z_n = 5 * (1 - send_a), 5 * (1 - recv_a), 5 * recv_a

    def first_tile(q, is_a):
        return 3 * FIRST[q] + 1 - is_a

    barrier = pltpu.get_barrier_semaphore()

    def greet(device):
        pl.semaphore_signal(barrier, inc=1, device_id=device, device_id_type=MESH)

    for d in FAR_FIRST:
        greet(across_z(d))
        greet(across_plane(d))
        if d:
            greet(z_peer(d))
            greet(plane_peer(d))
    greet(sibling)

    loads = [
        pltpu.make_async_copy(src, dst, load_sem.at[i])
        for i, (src, dst) in enumerate(
            [
                (inputs_hbm.at[0], inputs_ref),
                (active_hbm.at[0], active_ref),
                (goals_hbm, goals_ref),
                (enc_hbm.at[0], enc),
                (dec_hbm.at[0], dec),
            ]
        )
    ]
    for load in loads:
        load.start()

    xstage[...] = jnp.zeros_like(xstage)
    loads[0].wait()
    for c in range(TILES):
        xstage[2 * c : 2 * c + 2, :] = inputs_ref[:, c * LANES : (c + 1) * LANES].astype(F32)
    xz[z] = xstage[...].astype(BF16)

    pl.semaphore_wait(barrier, 31)

    def send(src, dst, ssem, rsem, device):
        pltpu.make_async_remote_copy(
            src_ref=src, dst_ref=dst, send_sem=ssem, recv_sem=rsem, device_id=device, device_id_type=MESH
        ).start()

    def wait(ref, sem):
        pltpu.make_async_copy(ref, ref, sem).wait()

    class Spread:
        def __init__(self, buf, half, near, mate, ssem, rsem, direct):
            self.buf, self.half, self.near, self.mate = buf, half, near, mate
            self.direct = direct
            self.ssem, self.rsem = ssem, rsem

        def put(self, block, slot, device):
            send(self.buf.at[block], self.buf.at[block], self.ssem, self.rsem(slot), device)

        def put_half(self, block, i, slot, device):
            part_of = self.half(block, i)
            send(part_of, part_of, self.ssem, self.rsem(slot), device)

        def got(self, slot):
            wait(self.buf.at[0], self.rsem(slot))

        def start(self):
            own = y * 2 + self.near
            self.put(own, 1, right)
            self.put(own, 2, left)
            if self.direct:
                self.put(own, 3, right_pair)
                self.put(own, 4, left_pair)
            self.put(own, 0, pair)

        def from_pair(self):
            self.got(0)
            self.put(y * 2 + self.mate, 3, right)
            self.put(y * 2 + self.mate, 4, left)

        def onward(self, which, slot):
            self.got(slot)
            self.put_half(y3 * 2 + which, 0, slot + 4, right)
            self.got(slot + 1)
            self.put_half(y1 * 2 + which, 1, slot + 5, left)

        def second(self):
            self.onward(self.near, 1)

        def third(self):
            self.onward(self.mate, 3)

        def near_rows(self):
            if self.direct:
                self.got(0)

        def far_row(self):
            for slot in range(5, 9):
                wait(self.half(0, 0), self.rsem(slot))

        def finish(self):
            self.near_rows()
            self.far_row()

        def left_here(self):
            wait(self.buf.at[pl.ds(0, 7)], self.ssem)

    for d in FAR_FIRST[:7]:
        send(xz.at[z], xz.at[z], xz_send, xz_recv, z_peer(d))

    loads[1].wait()
    for gg in range(NG):
        for r in range(2):
            mask[gg * ROWS + r * 8 : gg * ROWS + r * 8 + 8, :] = active_ref[
                pl.ds(gg * 2 + r, 8, stride=16), :
            ].astype(F32)

    mine = lax.broadcasted_iota(jnp.int32, (8, 1), 0) == z
    loads[2].wait()

    first_half = (1 - x_hi).astype(F32)

    def goal_rows(target, tile, count, factor=first_half):
        two = goals_ref[target, :, cols(tile, count)].astype(F32) * factor
        zero = jnp.zeros((8, count * LANES), F32)
        return jnp.concatenate([jnp.where(mine, two[r : r + 1], zero) for r in range(2)], axis=0)

    t_a, t_b = 5 * x_hi + core, 2 + 2 * core
    for q, w in enumerate(TILES_OF):
        for zz in range(3):
            goal_block[q][zz] = goal_rows(t_a, 3 * FIRST[q] + w * zz, w, 1.0)
            goal_block[q][zz + 5] = goal_rows(t_b, 3 * FIRST[q] + 1 + w * zz, w)
        goal_block[q][MID] = goal_rows(3, core * 14 + FIRST[q], w)
    goal_block[0][MID + 1] = goal_rows(3, core * 14 + 9, 4)
    goal_block[1][MID + 1, :, 0:LANES] = goal_rows(3, core * 14 + 13, 1)
    goal_block[1][MID + 1, :, LANES : 2 * LANES] = goal_rows(t_a, 27, 1, 1.0)
    goal_block[1][MID + 1, :, 2 * LANES :] = goal_rows(t_b, 0, 1)
    goal_block[2][MID + 1] = jnp.zeros((ROWS, 2 * LANES), F32)

    wait(xz.at[pl.ds(0, 7)], xz_recv)
    for zz in range(NZ):
        xwide[zz * XROWS : (zz + 1) * XROWS, :] = xz[zz].astype(F32)
    for c in range(TILES):
        xb[g, c // 14, :, (c % 14) * LANES : (c % 14 + 1) * LANES] = jnp.concatenate(
            [xwide[pl.ds(2 * c + r, 8, stride=XROWS), :] for r in range(2)], axis=0
        ).astype(BF16)

    x_spread = Spread(xb, lambda b, i: xb.at[b, i], x, 1 - x, xb_send, lambda slot: xb_recv.at[slot], True)
    x_spread.start()
    x_spread.second()
    x_spread.third()
    loads[3].wait()
    loads[4].wait()
    x_spread.finish()

    pre = jnp.dot(xb[:, 0].reshape(TOK, D // 2), enc[: D // 2, :], preferred_element_type=F32)
    pre = pre + jnp.dot(xb[:, 1].reshape(TOK, D // 2), enc[D // 2 :, :], preferred_element_type=F32)
    act = mask[...] * pre
    lat_ref[...] = act.astype(BF16)
    latt_ref[...] = act.T.astype(BF16)

    def decoded(k, tile, count=3):
        return jnp.dot(lat_ref[...], dec[k, :, cols(tile, count)], preferred_element_type=F32)

    def blocks(value):
        return value.reshape(NG, ROWS, value.shape[-1])

    other = (1 - core) * 14
    own = core * 14
    is_a, is_b = send_a.astype(F32), (1 - send_a).astype(F32)
    empty = jnp.zeros((NG, ROWS, 2 * LANES), BF16)

    def cut(value, q, i):
        w = TILES_OF[q] * LANES
        return blocks(value[:, i * w : (i + 1) * w])

    def for_sibling(q):
        w = TILES_OF[q]
        wide = decoded(k_s, first_tile(q, send_a), 3 * w).astype(BF16)
        for i in range(3):
            sib_out[q][i] = cut(wide, q, i)
        sib_out[q][3] = blocks(decoded(k_c, other + FIRST[q], w).astype(BF16))
        if q == 0:
            sib_out[q][4] = blocks(decoded(k_c, other + 9, 4).astype(BF16))
        elif q == 1:
            sib_out[q][4, :, :, 0:LANES] = blocks(decoded(k_c, other + 13, 1).astype(BF16))
            sib_out[q][4, :, :, LANES : 2 * LANES] = blocks((decoded(k_s, 27, 1) * is_a).astype(BF16))
            sib_out[q][4, :, :, 2 * LANES :] = blocks((decoded(k_s, 0, 1) * is_b).astype(BF16))
        else:
            sib_out[q][4] = empty
        send(sib_out[q], sib_in[q], sib_send.at[q], sib_recv.at[q], sibling)

    def own_alone(q):
        wide = decoded(k_n, first_tile(q, 1 - recv_a), 3 * TILES_OF[q]).astype(BF16)
        for i in range(3):
            part[q][:, z_n + i] = cut(wide, q, i)

    def own_shared(q):
        wait(sib_in[q], sib_recv.at[q])
        w = TILES_OF[q]
        wide = decoded(k_r, first_tile(q, recv_a), 3 * w)
        for i in range(3):
            part[q][:, z_r + i] = (cut(wide, q, i) + sib_in[q][i].astype(F32)).astype(BF16)
        part[q][:, MID] = (blocks(decoded(k_c, own + FIRST[q], w)) + sib_in[q][3].astype(F32)).astype(BF16)

        def last(lanes, value):
            part[q][:, MID + 1, :, lanes] = (blocks(value) + sib_in[q][4, :, :, lanes].astype(F32)).astype(BF16)

        if q == 0:
            last(slice(0, 4 * LANES), decoded(k_c, own + 9, 4))
        elif q == 1:
            last(slice(0, LANES), decoded(k_c, own + 13, 1))
            last(slice(LANES, 2 * LANES), decoded(k_a, 27, 1))
            last(slice(2 * LANES, 3 * LANES), decoded(k_b, 0, 1))
        else:
            part[q][:, MID + 1] = empty

    def less_goals(q):
        for zz in range(NZ):
            part[q][g, zz] = (part[q][g, zz].astype(F32) - goal_block[q][zz]).astype(BF16)

    def y_first(q):
        ss = y_send.at[0]
        send(part[q].at[y2 * 2], y_in.at[0], ss, y_recv.at[0, 0], right)
        send(part[q].at[y2 * 2 + 1], y_in.at[1], ss, y_recv.at[0, 1], left)
        send(part[q].at[y1 * 2 + 1], y_in.at[2], ss, y_recv.at[0, 2], right)
        send(part[q].at[y3 * 2], y_in.at[3], ss, y_recv.at[0, 2], left)

    def y_second(q):
        ss = y_send.at[0]
        wait(y_in.at[0], y_recv.at[0, 0])
        for zz in range(NZ):
            part[q][y1 * 2, zz] = (part[q][y1 * 2, zz].astype(F32) + y_in[0, zz].astype(F32)).astype(BF16)
        send(part[q].at[y1 * 2], y_in.at[4], ss, y_recv.at[0, 2], right)
        wait(y_in.at[1], y_recv.at[0, 1])
        for zz in range(NZ):
            part[q][y3 * 2 + 1, zz] = (
                part[q][y3 * 2 + 1, zz].astype(F32) + y_in[1, zz].astype(F32)
            ).astype(BF16)
        send(part[q].at[y3 * 2 + 1], y_in.at[5], ss, y_recv.at[0, 2], left)

    def y_sum(q):
        wait(y_in.at[pl.ds(0, 4)], y_recv.at[0, 2])
        for half, (one, two) in enumerate(((3, 4), (2, 5))):
            here = (x == half).astype(F32)
            for zz in range(NZ):
                part[q][y * 2 + half, zz] = (
                    part[q][y * 2 + half, zz].astype(F32)
                    + y_in[one, zz].astype(F32)
                    + y_in[two, zz].astype(F32)
                    - goal_block[q][zz] * here
                ).astype(BF16)
        send(part[q].at[g_pass], x_in, x_send.at[0], x_recv.at[0], pair)

    def to_z(q):
        for d in FAR_FIRST[:7]:
            send(part[q].at[g_keep, (z + d) % NZ], z_in[q].at[d - 1], z_send.at[q], z_recv.at[q], z_peer(d))

    def x_sum(q):
        wait(x_in, x_recv.at[0])
        for zz in range(NZ):
            part[q][g_keep, zz] = (part[q][g_keep, zz].astype(F32) + x_in[zz].astype(F32)).astype(BF16)
        to_z(q)

    def pair_first():
        less_goals(1)
        for j in (2, 1, 3, 0):
            send(
                part[1].at[((y + j) % 4) * 2 + 1 - keep], pair_in.at[j], x_send.at[1], pair_recv.at[j], pair
            )

    def pair_sum(j):
        wait(pair_in.at[j], pair_recv.at[j])
        to = ((y + j) % 4) * 2 + keep
        for zz in range(NZ):
            part[1][to, zz] = (part[1][to, zz].astype(F32) + pair_in[j, zz].astype(F32)).astype(BF16)

    low, high = pl.ds(0, 4), pl.ds(4, 4)

    def half_far():
        ss = y_send.at[1]
        pair_sum(2)
        send(part[1].at[y2 * 2 + keep, low], half_in.at[0], ss, y_recv.at[1, 0], right)
        send(part[1].at[y2 * 2 + keep, high], half_in.at[1], ss, y_recv.at[1, 1], left)

    def half_near():
        ss = y_send.at[1]
        pair_sum(1)
        send(part[1].at[y1 * 2 + keep, high], half_in.at[2], ss, y_recv.at[1, 2], right)
        pair_sum(3)
        send(part[1].at[y3 * 2 + keep, low], half_in.at[3], ss, y_recv.at[1, 2], left)

    def half_second():
        ss = y_send.at[1]
        wait(half_in.at[0], y_recv.at[1, 0])
        to = y1 * 2 + keep
        for zz in range(4):
            part[1][to, zz] = (part[1][to, zz].astype(F32) + half_in[0, zz].astype(F32)).astype(BF16)
        send(part[1].at[to, low], half_in.at[4], ss, y_recv.at[1, 2], right)
        wait(half_in.at[1], y_recv.at[1, 1])
        to = y3 * 2 + keep
        for zz in range(4):
            part[1][to, zz + 4] = (part[1][to, zz + 4].astype(F32) + half_in[1, zz].astype(F32)).astype(BF16)
        send(part[1].at[to, high], half_in.at[5], ss, y_recv.at[1, 2], left)

    def half_sum():
        pair_sum(0)
        wait(half_in.at[pl.ds(0, 4)], y_recv.at[1, 2])
        for at, one, two in ((0, 3, 4), (4, 2, 5)):
            for zz in range(4):
                part[1][g_keep, at + zz] = (
                    part[1][g_keep, at + zz].astype(F32)
                    + half_in[one, zz].astype(F32)
                    + half_in[two, zz].astype(F32)
                ).astype(BF16)
        to_z(1)

    def z_sum(q):
        wait(z_in[q], z_recv.at[q])
        total = part[q][g_keep, z].astype(F32)
        for i in range(7):
            total = total + z_in[q][i].astype(F32)
        value = (total * scale).astype(BF16)
        term[q][...] = value
        err[q][g_keep, z] = value
        own = term[q]
        for d in FAR_FIRST[:7]:
            send(own, err[q].at[g_keep, z], ez_send.at[q], ez_recv.at[q], z_peer(d))

        @pl.when(z >= 3)
        def _():
            for d in FAR_FIRST:
                send(own, err_far[q].at[z - 3], ef_send.at[q], ef_recv.at[q], across_z(d))

    def bulk_first():
        less_goals(2)
        for d in FAR_FIRST[:7]:
            send(part[2].at[:, (z + d) % NZ], bulk_in.at[d - 1], bulk_send.at[0], bulk_recv.at[0], z_peer(d))

    def bulk_sum():
        wait(bulk_in, bulk_recv.at[0])
        for gg in range(NG):
            total = part[2][gg, z].astype(F32)
            for i in range(7):
                total = total + bulk_in[i, gg].astype(F32)
            part[2][gg, z] = total.astype(BF16)
        for d in range(1, 8):
            send(
                part[2].at[(g + d) % NG, z], plane_in.at[d - 1], plane_send.at[0], plane_recv.at[0], plane_peer(d)
            )

    def plane_sum():
        wait(plane_in, plane_recv.at[0])
        total = part[2][g, z].astype(F32)
        for i in range(7):
            total = total + plane_in[i].astype(F32)
        value = (total * scale).astype(BF16)
        term[2][...] = value
        err[2][g, z] = value
        own = term[2]
        for d in range(1, 8):
            send(own, err[2].at[g, z], plane_send.at[1], plane_recv.at[1], plane_peer(d))

        @pl.when(z >= 3)
        def _():
            for d in FAR_FIRST:
                send(own, plane_far.at[g], far_send, far_recv, across_plane(d))

    def plane_spread():
        wait(plane_in, plane_recv.at[1])

        @pl.when(z >= 3)
        def _():
            wait(plane_far, far_recv)
            for gg in range(NG):
                err[2][gg, z] = (err[2][gg, z].astype(F32) + plane_far[gg].astype(F32)).astype(BF16)

        for d in FAR_FIRST[:7]:
            send(err[2].at[:, z], err[2].at[:, z], bulk_send.at[1], bulk_recv.at[1], z_peer(d))

    def to_sibling(q):
        send(err[q].at[:, pl.ds(z_r, 3)], err_sib[q].at[:, pl.ds(0, 3)], es_send.at[q], es_recv.at[q], sibling)
        send(err[q].at[:, pl.ds(3, 2)], err_sib[q].at[:, pl.ds(3, 2)], es_send.at[q], es_recv.at[q], sibling)

    def bulk_arrived():
        wait(bulk_in, bulk_recv.at[1])
        to_sibling(2)

    y_spread = Spread(
        err[0],
        lambda b, i: err[0].at[b, pl.ds(4 * i, 4)],
        keep,
        1 - keep,
        ep_send.at[0],
        lambda slot: ep_recv.at[0, slot],
        False,
    )

    class HalfSpread:
        def put(self, block, which, slot, device):
            at = err[1].at[block] if which is None else err[1].at[block, which]
            send(at, at, ep_send.at[1], ep_recv.at[1, slot], device)

        def got(self, slot, which=None):
            wait(err[1].at[0] if which is None else err[1].at[0, which], ep_recv.at[1, slot])

        def start(self):
            self.put(g_keep, None, 0, right)
            self.put(g_keep, None, 1, left)
            self.put(g_keep, None, 4, pair)

        def second(self):
            self.got(0)
            self.put(y3 * 2 + keep, low, 2, right)
            self.put(y3 * 2 + keep, None, 5, pair)
            self.got(1)
            self.put(y1 * 2 + keep, high, 3, left)
            self.put(y1 * 2 + keep, None, 6, pair)

        def third(self):
            self.got(2, low)
            self.put(y2 * 2 + keep, low, 7, pair)
            self.got(3, high)
            self.put(y2 * 2 + keep, high, 8, pair)

        def near_rows(self):
            for slot in (4, 5, 6):
                self.got(slot)

        def far_row(self):
            self.got(7, low)
            self.got(8, high)

        def left_here(self):
            wait(err[1].at[pl.ds(0, 7)], ep_send.at[1])

    spreads = [y_spread, HalfSpread()]

    def z_spread(q):
        wait(err[q].at[0, pl.ds(0, 7)], ez_recv.at[q])
        wait(err_far[q], ef_recv.at[q])
        for zz in range(3, NZ):
            far = err_far[q][zz - 3].astype(F32)
            if q == 1 and zz == 4:
                tile = lax.broadcasted_iota(jnp.int32, (ROWS, 3 * LANES), 1) // LANES
                far = jnp.where(tile == 1, 0.0, far)
            err[q][g_keep, zz] = (err[q][g_keep, zz].astype(F32) + far).astype(BF16)
        spreads[q].start()

    def row_to_sibling(q, row):
        rows = pl.ds(2 * row, 2)
        send(err[q].at[rows, pl.ds(z_r, 3)], err_sib[q].at[rows, pl.ds(0, 3)], es_send.at[q], es_recv.at[q], sibling)
        send(err[q].at[rows, pl.ds(3, 2)], err_sib[q].at[rows, pl.ds(3, 2)], es_send.at[q], es_recv.at[q], sibling)

    def near_arrived(q):
        spreads[q].near_rows()
        for row in (y, y1, y3):
            row_to_sibling(q, row)

    def arrived(q):
        spreads[q].far_row()
        row_to_sibling(q, y2)

    def backward(error, k, tile, count=3):
        where = cols(tile, count)
        dlat_ref[...] += lax.dot_general(
            error, dec[k, :, where], (((1,), (1,)), ((), ())), preferred_element_type=F32
        )
        gdec[k, :, where] = jnp.dot(latt_ref[...], error, preferred_element_type=F32).astype(BF16)

    def whole(value):
        return value.reshape(TOK, value.shape[-1])

    def wide(ref, q, at):
        return jnp.concatenate([whole(ref[q][:, at + i]) for i in range(3)], axis=1)

    def own_back(q):
        w = TILES_OF[q]
        backward(wide(err, q, 0), k_a, first_tile(q, 1), 3 * w)
        backward(wide(err, q, 5), k_b, first_tile(q, 0), 3 * w)
        backward(whole(err[q][:, MID]), k_c, own + FIRST[q], w)
        if q == 0:
            backward(whole(err[q][:, MID + 1]), k_c, own + 9, 4)
        elif q == 1:
            backward(whole(err[q][:, MID + 1, :, 0:LANES]), k_c, own + 13, 1)
            backward(whole(err[q][:, MID + 1, :, LANES : 2 * LANES]), k_a, 27, 1)
            backward(whole(err[q][:, MID + 1, :, 2 * LANES :]), k_b, 0, 1)

    def sibling_back(q):
        wait(err_sib[q], es_recv.at[q])
        w = TILES_OF[q]
        backward(wide(err_sib, q, 0), k_s, first_tile(q, send_a), 3 * w)
        backward(whole(err_sib[q][:, 3]), k_c, other + FIRST[q], w)
        if q == 0:
            backward(whole(err_sib[q][:, 4]), k_c, other + 9, 4)
        elif q == 1:
            backward(whole(err_sib[q][:, 4, :, 0:LANES]), k_c, other + 13, 1)
            lanes = pl.ds(pl.multiple_of((2 - send_a) * LANES, LANES), LANES)
            backward(whole(err_sib[q][:, 4, :, lanes]), k_s, 27 * send_a, 1)

    for_sibling(1)
    for_sibling(0)
    own_alone(1)
    own_shared(1)
    pair_first()
    for_sibling(2)
    own_alone(0)
    own_shared(0)
    y_first(0)
    own_alone(2)
    own_shared(2)
    bulk_first()
    half_far()
    half_near()
    y_second(0)
    half_second()
    y_sum(0)
    half_sum()
    x_sum(0)
    for c in range(TILES):
        block = xb[:, c // 14, :, (c % 14) * LANES : (c % 14 + 1) * LANES].reshape(TOK, LANES)
        xt[c * LANES : (c + 1) * LANES, :] = block.T
    dlat_ref[...] = jnp.zeros_like(dlat_ref)
    z_sum(1)
    bulk_sum()
    z_sum(0)
    plane_sum()
    z_spread(1)
    z_spread(0)
    plane_spread()
    spreads[1].second()
    spreads[0].from_pair()
    spreads[1].third()
    near_arrived(1)
    spreads[0].second()
    spreads[0].third()
    near_arrived(0)
    arrived(1)
    bulk_arrived()
    own_back(1)
    own_back(2)
    sibling_back(1)
    arrived(0)
    own_back(0)
    sibling_back(2)
    sibling_back(0)

    wait(xz.at[pl.ds(0, 7)], xz_send)
    x_spread.left_here()
    for q in range(NQ):
        wait(sib_in[q], sib_send.at[q])
        wait(err_sib[q], es_send.at[q])
    for q in range(2):
        wait(z_in[q], z_send.at[q])
        wait(z_in[q], ez_send.at[q])
        spreads[q].left_here()
    wait(y_in, y_send.at[0])
    wait(half_in, y_send.at[1])
    wait(x_in, x_send.at[0])
    wait(pair_in, x_send.at[1])
    for i in range(2):
        wait(bulk_in, bulk_send.at[i])
        wait(plane_in, plane_send.at[i])

    @pl.when(z >= 3)
    def _():
        for q in range(2):
            wait(err[q].at[0], ef_send.at[q])
        wait(plane_far, far_send)


def last_kernel(gdec, xt, mask, dlat, genc_hbm, gdec_hbm, genc, sem):
    gdec_copy = pltpu.make_async_copy(gdec, gdec_hbm.at[0], sem.at[0])
    gdec_copy.start()
    dpre = (mask[...] * dlat[...]).astype(BF16)
    genc[...] = jnp.dot(xt[...], dpre, preferred_element_type=F32).astype(BF16)
    genc_copy = pltpu.make_async_copy(genc, genc_hbm.at[0], sem.at[1])
    genc_copy.start()
    gdec_copy.wait()
    genc_copy.wait()


def local(inputs, encoder, active, decoder, goals):
    vmem = pl.BlockSpec(memory_space=pltpu.VMEM)
    hbm = pl.BlockSpec(memory_space=pl.ANY)
    dma = pltpu.SemaphoreType.DMA
    per_q = [dma((NQ,))] * 2

    def chunk(q, shape, dtype=BF16):
        return pltpu.VMEM((*shape, TILES_OF[q] * LANES), dtype)

    def chunks(shape, dtype=BF16):
        return [chunk(q, shape, dtype) for q in range(NQ)]

    gdec, xt, mask, dlat = pl.pallas_call(
        kernel,
        out_shape=(
            pltpu.VMEM((4, FL, D), BF16),
            pltpu.VMEM((D, TOK), BF16),
            pltpu.VMEM((TOK, FL), F32),
            pltpu.VMEM((TOK, FL), F32),
        ),
        in_specs=[pl.BlockSpec(memory_space=pltpu.HBM)] * 5,
        out_specs=[vmem] * 4,
        scratch_shapes=[
            pltpu.VMEM((2, D), BF16),
            pltpu.VMEM((7, 2, D), BF16),
            pltpu.VMEM((TOK, FL), jnp.int32),
            pltpu.VMEM((D, FL), BF16),
            pltpu.VMEM((4, FL, D), BF16),
            pltpu.VMEM((XROWS, LANES), F32),
            pltpu.VMEM((NZ, XROWS, LANES), BF16),
            pltpu.VMEM((NZ * XROWS, LANES), F32),
            pltpu.VMEM((NG, 2, ROWS, D // 2), BF16),
            pltpu.VMEM((TOK, FL), BF16),
            pltpu.VMEM((FL, TOK), BF16),
            chunks((NZ, ROWS), F32),
            chunks((5, NG, ROWS)),
            chunks((5, NG, ROWS)),
            chunks((NG, NZ, ROWS)),
            chunk(0, (6, NZ, ROWS)),
            chunk(1, (6, 4, ROWS)),
            chunk(1, (4, NZ, ROWS)),
            chunk(0, (NZ, ROWS)),
            chunks((NZ - 1, ROWS))[:2],
            chunk(2, (NZ - 1, NG, ROWS)),
            chunk(2, (NG - 1, ROWS)),
            chunks((ROWS,)),
            chunks((NG, NZ, ROWS)),
            chunks((5, ROWS))[:2],
            chunk(2, (NG, ROWS)),
            chunks((NG, 5, ROWS)),
            dma((5,)),
            dma,
            dma,
            dma,
            dma((9,)),
            *per_q,
            dma((NQ,)),
            dma((NQ, 3)),
            *per_q,
            dma((4,)),
            *per_q,
            *per_q,
            *per_q,
            dma((NQ,)),
            dma((NQ, 9)),
            *per_q,
            dma((2,)),
            dma((2,)),
            dma((2,)),
            dma((2,)),
            dma,
            dma,
        ],
        compiler_params=pltpu.CompilerParams(
            collective_id=0, has_side_effects=True, vmem_limit_bytes=54 * 2**20
        ),
        name="step",
    )(inputs, goals, active, encoder, decoder)
    return pl.pallas_call(
        last_kernel,
        out_shape=(
            jax.ShapeDtypeStruct((1, D, FL), BF16),
            jax.ShapeDtypeStruct((1, 4, FL, D), BF16),
        ),
        in_specs=[vmem] * 4,
        out_specs=(hbm, hbm),
        scratch_shapes=[pltpu.VMEM((D, FL), BF16), dma((2,))],
        compiler_params=pltpu.CompilerParams(vmem_limit_bytes=8 * 2**20),
        name="write",
    )(gdec, xt, mask, dlat)


def solution(mesh):
    return jax.shard_map(
        local,
        mesh=mesh,
        in_specs=(
            P("layer", "slab", None),
            P("layer", None, "slab"),
            P("layer", None, "slab"),
            P("layer", None, "slab", None),
            P(None, "slab", None),
        ),
        out_specs=(P("layer", None, "slab"), P("layer", None, "slab", None)),
        check_vma=False,
    )
```
